128 devices in a mesh: len: 8 (over y, core), hgt: 16 (over x, z).
Axes of the slice: x: 4, y: 4, z: 4, core: 2. Of those that a mesh axis runs over, the one named last changes fastest.
Arguments:
- air_temp: float32 [64, 128, 256], P('len', 'hgt'), may hold values from -6 to 6
- velocity: float32 [64, 128, 256], P('len', 'hgt'), may hold values from -1 to 1
- fluid: int32 [64, 128, 256], P('len', 'hgt'), may hold values 0 or 1
- enthalpy: float32 [4096, 128], P(('len', 'hgt')), may hold values from -1 to 3
- adjacency_lists: int32 [4096, 8, 128], P(('len', 'hgt')), may hold values from 0 to 127
- send_cells: int32 [128, 128, 256], P(('len', 'hgt')), may hold values from 0 to 16383
- contact: float32 [128, 128, 256], P(('len', 'hgt')), may hold values from 0.2 to 2
- pair_rows: int32 [128, 128], P(('len', 'hgt')), may hold values from 0 to 256, as said below
- recv_nodes: int32 [128, 128, 256], P(('len', 'hgt')), may hold values from 0 to 4095
Outputs:
- air_out: float32 [64, 128, 256], P('len', 'hgt')
- enthalpy_out: float32 [4096, 128], P(('len', 'hgt'))
The draws below stay inside these ranges and needn't reach their ends.
Inputs may be any that keep to these rules, and one draw needn't show every extreme that they name: Rows 0 to pair_rows[s, d] - 1 of pair (s, d) are live, the others are padding. In every draw one owner receives 256 live rows from every air device; other owners receive fewer.
All inputs are finite; a program needn't handle non-finite values. No bound on the sum of `fluid` on one device may be relied on, other than what follows from the above.
Results may differ from the reference program's by a relative error of at most 0.0003.
Values sent between devices are 32-bit elements; how exact they have to be, the bound alone decides.
No kernel may reach another device: no remote copies, remote signals or barrier semaphores. Data moves between devices by JAX's collectives and lax.ppermute only.
A program may use at most 64 MiB of HBM per device.

```python
import math
import jax
import jax.numpy as jnp

CL = 8
CH = 8
CW = 256
PANELS_PER_UNIT = 32
PANEL_HEIGHT = 128
K = 8
PROCESSOR_COUNT = 128
NL = 64
NH = 128
PAIR = 256
NODEBLKS = 4096
N_LEN = 8
N_HGT = 16


def draw_pair_rows(key, part):
    first, second, third = jax.random.split(jax.random.fold_in(key, 17), 3)
    reach = jax.random.randint(first, (PROCESSOR_COUNT,), PAIR // 2, PAIR + 1)
    counts = jax.random.randint(second, (PROCESSOR_COUNT, PROCESSOR_COUNT), PAIR // 4, PAIR + 1)
    counts = counts * reach[None, :] // PAIR
    fullest = jax.random.randint(third, (), 0, PROCESSOR_COUNT)
    columns = jnp.arange(PROCESSOR_COUNT)[None, :]
    return jnp.where(columns == fullest, PAIR, counts).astype(jnp.int32)


def place_ends(values, key, least, high):
    extent = values.shape
    spot = [jax.random.randint(jax.random.fold_in(key, axis), (), 0, extent[axis]) for axis in range(len(extent))]
    values = values.at[tuple(spot)].set(least)
    longest = extent.index(max(extent))
    spot[longest] = (spot[longest] + 1) % extent[longest]
    return values.at[tuple(spot)].set(high)


def block_levels(stream_key, extent, pieces, low, top_value):
    factor_of = 1.0
    for axis_at, blocks in pieces:
        draws = jax.random.uniform(jax.random.fold_in(jax.random.fold_in(stream_key, 6), axis_at), (blocks,), jnp.float32, low / len(pieces), top_value / len(pieces))
        factor_of = factor_of * jnp.repeat(jnp.exp(draws), extent[axis_at] // blocks).reshape((-1,) + (1,) * (len(extent) - 1 - axis_at))
    return factor_of


def noise(key, extent, width, bound, cuts=(), kind=jnp.bfloat16):
    factor_of = block_levels(key, extent, cuts, -0.22, 0.18) if cuts else 1.0
    result = jax.random.normal(key, extent, jnp.float32) * width * factor_of
    return jnp.minimum(jnp.maximum(result, -bound), bound).astype(kind)


def setup_inputs(seed: int = 0) -> dict:
    seeds = jax.random.split(jax.random.key(seed), 10)
    return {
        "air_temp": noise(seeds[0], (NL, NH, CW), 1.0, 6.0, ((0, 8), (1, 16)), jnp.float32),
        "velocity": jnp.clip(jax.random.uniform(seeds[1], (NL, NH, CW), jnp.float32, -1.0, 1.0) * block_levels(seeds[1], (NL, NH, CW), ((0, 8), (1, 16)), -0.4, 0.0), -1.0, 1.0),
        "fluid": place_ends((jax.random.randint(seeds[2], (NL, NH, CW), 0, 8) < 7).astype(jnp.int32), jax.random.fold_in(seeds[2], 1), 0, 1),
        "enthalpy": jnp.clip(-1.0 + 4.0 * jax.random.uniform(seeds[3], (NODEBLKS, PANEL_HEIGHT), jnp.float32) ** block_levels(seeds[3], (NODEBLKS, PANEL_HEIGHT), ((0, 128),), -0.2, 0.2), -1.0, 3.0),
        "adjacency_lists": place_ends(jax.random.randint(seeds[4], (NODEBLKS, K, PANEL_HEIGHT), 0, PANEL_HEIGHT), jax.random.fold_in(seeds[4], 1), 0, PANEL_HEIGHT - 1).astype(jnp.int32),
        "send_cells": place_ends(jax.random.randint(seeds[5], (PROCESSOR_COUNT, PROCESSOR_COUNT, PAIR), 0, min(CL * CH * CW, 65536)), jax.random.fold_in(seeds[5], 1), 0, (min(CL * CH * CW, 65536)) - 1).astype(jnp.int32),
        "contact": jnp.clip(jnp.exp(math.log(2.0) - 2.3025851 * jax.random.uniform(seeds[6], (PROCESSOR_COUNT, PROCESSOR_COUNT, PAIR), jnp.float32) ** block_levels(seeds[6], (PROCESSOR_COUNT, PROCESSOR_COUNT, PAIR), ((0, 128),), -0.2, 0.2)), 0.2, 2.0),
        "pair_rows": draw_pair_rows(jax.random.fold_in(seeds[9], 71), 0),
        "recv_nodes": place_ends(jax.random.randint(seeds[8], (PROCESSOR_COUNT, PROCESSOR_COUNT, PAIR), 0, PANELS_PER_UNIT * PANEL_HEIGHT), jax.random.fold_in(seeds[8], 1), 0, (PANELS_PER_UNIT * PANEL_HEIGHT) - 1).astype(jnp.int32),
    }


LATENT = 1.0
SOLID_SLOPE = 2.0
DT_AIR = 0.1
DT_NODE = 0.05


def warmth_per_point(matrix_coefficients):
    return jnp.where(matrix_coefficients < 0.0, SOLID_SLOPE * matrix_coefficients, jnp.where(matrix_coefficients > LATENT, matrix_coefficients - LATENT, 0.0))


def to_blocks(field):
    return field.reshape(N_LEN, CL, N_HGT, CH, CW).transpose(0, 2, 1, 3, 4).reshape(PROCESSOR_COUNT, CL * CH * CW)


def from_blocks(blocks):
    return blocks.reshape(N_LEN, N_HGT, CL, CH, CW).transpose(0, 2, 1, 3, 4).reshape(NL, NH, CW)


def select_rows(matrix_coefficients, indices):
    return matrix_coefficients[indices]


def spread_rows(matrix_coefficients, indices, count):
    return jax.ops.segment_sum(matrix_coefficients.reshape(-1), indices.reshape(-1), num_segments=count)


def air_update(temper, velocity, fluid_f, source):
    padded = jnp.pad(temper, 1)
    behind = padded[:-2, 1:-1, 1:-1]
    ahead = padded[2:, 1:-1, 1:-1]
    laplace = ahead + behind + padded[1:-1, 2:, 1:-1] + padded[1:-1, :-2, 1:-1]
    laplace = laplace + padded[1:-1, 1:-1, 2:] + padded[1:-1, 1:-1, :-2] - 6.0 * temper
    advect = jnp.maximum(velocity, 0.0) * (temper - behind) + jnp.minimum(velocity, 0.0) * (ahead - temper)
    return temper + fluid_f * DT_AIR * (laplace - advect + source)


def reference(air_temp, velocity, fluid, enthalpy, adjacency_lists, send_cells, contact, pair_rows, recv_nodes):
    fluid_f = fluid.astype(jnp.float32)
    live_rows = jnp.arange(PAIR)[None, None, :] < pair_rows[:, :, None]
    weight = jnp.where(live_rows, contact, jnp.float32(0.0))
    temper = air_temp
    heat_content_sum = enthalpy
    for repeat in range(2):
        blocks = to_blocks(temper)
        sampled = jax.vmap(select_rows)(blocks, send_cells)
        meat_point_warmth = warmth_per_point(heat_content_sum)
        local_panel_share = meat_point_warmth.reshape(PROCESSOR_COUNT, PANELS_PER_UNIT * PANEL_HEIGHT)
        surface_boundary = jax.vmap(select_rows)(local_panel_share, recv_nodes)
        flux_row = weight.transpose(1, 0, 2) * (sampled.transpose(1, 0, 2) - surface_boundary)
        node_flux = jax.vmap(lambda matrix_coefficients, indices: spread_rows(matrix_coefficients, indices, PANELS_PER_UNIT * PANEL_HEIGHT))(flux_row, recv_nodes)
        collected_neighbour_data = jnp.take_along_axis(jnp.broadcast_to(meat_point_warmth[:, None, :], adjacency_lists.shape), adjacency_lists, axis=2)
        diffusive_flux = jnp.sum(collected_neighbour_data - meat_point_warmth[:, None, :], axis=1)
        heat_content_sum = heat_content_sum + DT_NODE * (diffusive_flux + node_flux.reshape(NODEBLKS, PANEL_HEIGHT))
        src_row = weight * (surface_boundary.transpose(1, 0, 2) - sampled)
        source = jax.vmap(lambda matrix_coefficients, indices: spread_rows(matrix_coefficients, indices, CL * CH * CW))(src_row, send_cells)
        temper = air_update(temper, velocity, fluid_f, from_blocks(source))
    return temper, heat_content_sum
```

```python
import jax
import jax.numpy as jnp
from jax import lax
from jax.experimental import pallas as pl
from jax.experimental.pallas import tpu as pltpu
from jax.sharding import PartitionSpec as P

LATENT = 1.0
SOLID_SLOPE = 2.0
DT_AIR = 0.1
DT_NODE = 0.05

F32 = jnp.float32
BF16 = jnp.bfloat16
I32 = jnp.int32
LANES = 128
PAIRS = 128
PAIR_ROWS = 256
GROUP = 16


def node_temp(enthalpy):
    return jnp.where(
        enthalpy < 0.0,
        SOLID_SLOPE * enthalpy,
        jnp.where(enthalpy > LATENT, enthalpy - LATENT, 0.0),
    )


def take(row, lane):
    return jnp.take_along_axis(jnp.broadcast_to(row, lane.shape), lane, axis=1)


def gather(rows, index):
    lane = index & (LANES - 1)
    high = index >> 7
    parts = [jnp.zeros(index.shape, F32) for _ in range(4)]
    for j, row in enumerate(rows):
        parts[j % 4] = jnp.where(high == j, take(row, lane), parts[j % 4])
    return (parts[0] + parts[1]) + (parts[2] + parts[3])


def air_rows(air_ref):
    return [
        air_ref[i, j : j + 1, h : h + LANES]
        for i in range(8)
        for j in range(8)
        for h in (0, LANES)
    ]


def iota16():
    return lax.broadcasted_iota(I32, (16, LANES), 0).astype(F32).astype(BF16)


def as_bf16(index):
    return index.astype(F32).astype(BF16)


def two_parts(value):
    top = value.astype(BF16)
    return top, (value - top.astype(F32)).astype(BF16)


def one_hot(index, count, iota):
    one = jnp.ones((16, LANES), BF16)
    zero = jnp.zeros((16, LANES), BF16)
    return jnp.concatenate(
        [jnp.where(index == iota + BF16(16 * i), one, zero) for i in range(count // 16)], axis=0
    )


def weighted(index, values, count, iota):
    zero = jnp.zeros((16, LANES), BF16)
    masks = [index == iota + BF16(16 * i) for i in range(count // 16)]
    return jnp.concatenate(
        [jnp.where(m, part, zero) for v in values for part in two_parts(v) for m in masks], axis=0
    )


def scatter(split, values, high_count, n_values, pairs=PAIRS, group=GROUP):
    iota = iota16()

    def body(g, acc):
        left, right = [], []
        for k in range(group):
            pair = (pl.multiple_of(g * group, group), k)
            for half in range(2):
                high, low = split(pair, half)
                left.append(weighted(as_bf16(high), values(pair, half), high_count, iota))
                right.append(one_hot(as_bf16(low), LANES, iota))
        left = jnp.concatenate(left, axis=1)
        right = jnp.concatenate(right, axis=1)
        return acc + lax.dot_general(
            left, right, (((1,), (1,)), ((), ())), preferred_element_type=F32
        )

    acc = lax.fori_loop(
        0, pairs // group, body, jnp.zeros((2 * n_values * high_count, LANES), F32)
    )
    out = []
    for n in range(n_values):
        at = 2 * n * high_count
        out.append(acc[at : at + high_count] + acc[at + high_count : at + 2 * high_count])
    return out


def lane_row(ref, row):
    return jnp.broadcast_to(ref[pl.ds(row, 1), :], (16, LANES))


def pair_row(ref, pair, half):
    start, k = pair
    view = ref.at[pl.ds(start, GROUP), half * LANES : (half + 1) * LANES]
    return jnp.broadcast_to(view[k : k + 1, :], (16, LANES))


def cell_split(cell_ref):
    def split(pair, half):
        cell = pair_row(cell_ref, pair, half)
        return ((cell >> 7) & 1) * 64 + (cell >> 8), cell & (LANES - 1)

    return split


def node_split(node_ref):
    def split(pair, half):
        node = pair_row(node_ref, pair, half)
        return node >> 7, node & (LANES - 1)

    return split


def to_block(table):
    return jnp.concatenate([table[:64], table[64:]], axis=1).reshape(8, 8, 256)


def pre_kernel(air_ref, enthalpy_ref, cell_ref, contact_ref, rows_ref, node_ref, out_ref, weight_ref):
    live = jnp.transpose(jnp.broadcast_to(rows_ref[...], (LANES, LANES)))
    for half in range(2):
        at = half * LANES
        spot = lax.broadcasted_iota(I32, (PAIRS, LANES), 1) + at
        weight_ref[:, at : at + LANES] = jnp.where(
            spot < live, contact_ref[:, at : at + LANES], 0.0
        )
    pack(air_ref, node_temp(enthalpy_ref[...]), cell_ref, weight_ref, node_ref, out_ref, True)


def pack(air_ref, warmth, cell_ref, weight_ref, node_ref, out_ref, with_weight):
    per_pair = 6 if with_weight else 4
    warm_rows = [warmth[j : j + 1] for j in range(warmth.shape[0])]
    table = air_rows(air_ref)

    def body(k, carry):
        at = pl.ds(pl.multiple_of(k * 8, 8), 8)
        for half in range(2):
            lanes = slice(half * LANES, (half + 1) * LANES)
            weight = weight_ref[at, lanes]
            base = k * 8 * per_pair + half
            out_ref[pl.ds(base, 8, stride=per_pair), :] = weight * gather(table, cell_ref[at, lanes])
            out_ref[pl.ds(base + 2, 8, stride=per_pair), :] = gather(warm_rows, node_ref[at, lanes])
            if with_weight:
                out_ref[pl.ds(base + 4, 8, stride=per_pair), :] = weight
        return carry

    lax.fori_loop(0, PAIRS // 8, body, 0)


def side_kernel(cell_ref, weight_ref, out_ref):
    (total,) = scatter(
        cell_split(cell_ref), lambda p, h: [pair_row(weight_ref, p, h)], 128, 1
    )
    out_ref[...] = to_block(total)


def conduction(warmth, links_ref):
    rows = []
    for b in range(warmth.shape[0]):
        linked = take(warmth[b : b + 1], links_ref[b])
        rows.append(jnp.sum(linked, axis=0, keepdims=True))
    return jnp.concatenate(rows, axis=0) - 8.0 * warmth


def air_step(air, velocity, fluid, behind_halo, ahead_halo, left_halo, right_halo, source):
    behind = jnp.concatenate([behind_halo, air[:-1]], axis=0)
    ahead = jnp.concatenate([air[1:], ahead_halo], axis=0)
    row = lax.broadcasted_iota(I32, air.shape, 1)
    lane = lax.broadcasted_iota(I32, air.shape, 2)
    low = jnp.where(row == 0, left_halo, pltpu.roll(air, 1, 1))
    high = jnp.where(row == 7, right_halo, pltpu.roll(air, 7, 1))
    flat = air.reshape(64, 256)
    left = jnp.where(lane == 0, 0.0, pltpu.roll(flat, 1, 1).reshape(air.shape))
    right = jnp.where(lane == 255, 0.0, pltpu.roll(flat, 255, 1).reshape(air.shape))
    laplace = (ahead + behind) + (high + low) + (right + left) - 6.0 * air
    advect = jnp.maximum(velocity, 0.0) * (air - behind) + jnp.minimum(velocity, 0.0) * (
        ahead - air
    )
    return air + fluid.astype(F32) * DT_AIR * (laplace - advect + source)


def step(
    received_ref, per_pair, air_ref, velocity_ref, fluid_ref, enthalpy_ref, links_ref, cell_ref,
    weight_ref, node_ref, behind_ref, ahead_ref, left_ref, right_ref, cell_total, node_total,
    air_out_ref, enthalpy_out_ref,
):
    def node_values(p, h):
        base = (p[0] + p[1]) * per_pair + h
        values = [lane_row(received_ref, base)]
        if node_total is None:
            values.append(lane_row(received_ref, base + 4))
        return values

    sums = scatter(node_split(node_ref), node_values, 32, 2 if node_total is None else 1)
    if node_total is None:
        node_total = sums[1]
    enthalpy = enthalpy_ref[...]
    warmth = node_temp(enthalpy)
    enthalpy_out_ref[...] = enthalpy + DT_NODE * (
        conduction(warmth, links_ref) + (sums[0] - warmth * node_total)
    )
    (heat,) = scatter(
        cell_split(cell_ref),
        lambda p, h: [pair_row(weight_ref, p, h) * lane_row(received_ref, (p[0] + p[1]) * per_pair + 2 + h)],
        128,
        1,
    )
    air = air_ref[...]
    air_out_ref[...] = air_step(
        air, velocity_ref[...], fluid_ref[...], behind_ref[...], ahead_ref[...], left_ref[...],
        right_ref[...], to_block(heat) - air * cell_total,
    )
    return node_total


def mid_kernel(
    received_ref, air_ref, velocity_ref, fluid_ref, enthalpy_ref, links_ref, cell_ref, weight_ref,
    node_ref, cell_total_ref, behind_ref, ahead_ref, left_ref, right_ref,
    air_out_ref, enthalpy_out_ref, node_total_ref, out_ref,
):
    node_total_ref[...] = step(
        received_ref, 6, air_ref, velocity_ref, fluid_ref, enthalpy_ref, links_ref, cell_ref,
        weight_ref, node_ref, behind_ref, ahead_ref, left_ref, right_ref, cell_total_ref[...], None,
        air_out_ref, enthalpy_out_ref,
    )
    pack(
        air_out_ref, node_temp(enthalpy_out_ref[...]), cell_ref, weight_ref, node_ref, out_ref, False
    )


def post_kernel(
    received_ref, air_ref, velocity_ref, fluid_ref, enthalpy_ref, links_ref, cell_ref, weight_ref,
    node_ref, cell_total_ref, node_total_ref, behind_ref, ahead_ref, left_ref, right_ref,
    air_out_ref, enthalpy_out_ref,
):
    step(
        received_ref, 4, air_ref, velocity_ref, fluid_ref, enthalpy_ref, links_ref, cell_ref,
        weight_ref, node_ref, behind_ref, ahead_ref, left_ref, right_ref, cell_total_ref[...],
        node_total_ref[...], air_out_ref, enthalpy_out_ref,
    )


def call(kernel, name, shapes):
    return pl.pallas_call(
        kernel,
        out_shape=[jax.ShapeDtypeStruct(s, F32) for s in shapes],
        name=name,
        compiler_params=pltpu.CompilerParams(vmem_limit_bytes=32 * 1024 * 1024),
    )


def halos(air):
    out = []
    for axis, dim in (("len", 0), ("hgt", 1)):
        count = lax.axis_size(axis)
        head = lax.slice_in_dim(air, 0, 1, axis=dim)
        tail = lax.slice_in_dim(air, air.shape[dim] - 1, air.shape[dim], axis=dim)
        out.append(lax.ppermute(tail, axis, [(i, i + 1) for i in range(count - 1)]))
        out.append(lax.ppermute(head, axis, [(i + 1, i) for i in range(count - 1)]))
    return out


def exchange(packed):
    both = packed.reshape(PAIRS, 1, -1)
    both = lax.all_to_all(both, ("len", "hgt"), split_axis=0, concat_axis=0, tiled=True)
    return both.reshape(packed.shape)


def local(
    air_temp, velocity, fluid, enthalpy, adjacency_lists, send_cells, contact, pair_rows, recv_nodes
):
    cells, nodes = send_cells[0], recv_nodes[0]
    block, panel, pairs = air_temp.shape, enthalpy.shape, cells.shape
    packed, weight = call(pre_kernel, "pack_first", [(6 * PAIRS, LANES), pairs])(
        air_temp, enthalpy, cells, contact[0], pair_rows, nodes
    )
    received = exchange(packed)
    edges = halos(air_temp)
    (cell_total,) = call(side_kernel, "cell_totals", [block])(cells, weight)
    air, heat, node_total, packed = call(
        mid_kernel, "first_step", [block, panel, panel, (4 * PAIRS, LANES)]
    )(
        received, air_temp, velocity, fluid, enthalpy, adjacency_lists, cells, weight, nodes,
        cell_total, *edges,
    )
    received = exchange(packed)
    edges = halos(air)
    air, heat = call(post_kernel, "second_step", [block, panel])(
        received, air, velocity, fluid, heat, adjacency_lists, cells, weight, nodes, cell_total,
        node_total, *edges,
    )
    return air, heat


def solution(mesh):
    rows = P(("len", "hgt"), None)
    lists = P(("len", "hgt"), None, None)
    grid = P("len", "hgt", None)
    in_specs = (grid, grid, grid, rows, lists, lists, lists, rows, lists)
    return jax.shard_map(
        local, mesh=mesh, in_specs=in_specs, out_specs=(grid, rows), check_vma=False
    )
```

```python
import jax
import jax.numpy as jnp
from jax import lax
from jax.experimental import pallas as pl
from jax.experimental.pallas import tpu as pltpu
from jax.sharding import PartitionSpec as P

LATENT = 1.0
SOLID_SLOPE = 2.0
DT_AIR = 0.1
DT_NODE = 0.05

F32 = jnp.float32
BF16 = jnp.bfloat16
I32 = jnp.int32
LANES = 128
PAIRS = 128
PAIR_ROWS = 256


def node_temp(enthalpy):
    return jnp.where(
        enthalpy < 0.0,
        SOLID_SLOPE * enthalpy,
        jnp.where(enthalpy > LATENT, enthalpy - LATENT, 0.0),
    )


def take(row, lane):
    return jnp.take_along_axis(jnp.broadcast_to(row, lane.shape), lane, axis=1)


def gather(rows, index):
    lane = index & (LANES - 1)
    bits = [((index >> (7 + b)) & 1) == 1 for b in range(len(rows).bit_length() - 1)]

    def pick(first, level):
        if level == 0:
            return take(rows[first], lane)
        low = pick(first, level - 1)
        high = pick(first + (1 << (level - 1)), level - 1)
        return jnp.where(bits[level - 1], high, low)

    return pick(0, len(bits))


def air_rows(air_ref):
    return [
        air_ref[i, j : j + 1, h : h + LANES]
        for i in range(8)
        for j in range(8)
        for h in (0, LANES)
    ]


def iota16():
    return lax.broadcasted_iota(I32, (16, LANES), 0).astype(F32).astype(BF16)


def as_bf16(index):
    return index.astype(F32).astype(BF16)


def two_parts(value):
    top = value.astype(BF16)
    return top, (value - top.astype(F32)).astype(BF16)


def one_hot(index, count, iota):
    one = jnp.ones((16, LANES), BF16)
    zero = jnp.zeros((16, LANES), BF16)
    return jnp.concatenate(
        [jnp.where(index == iota + BF16(16 * i), one, zero) for i in range(count // 16)], axis=0
    )


def weighted(index, values, count, iota):
    zero = jnp.zeros((16, LANES), BF16)
    masks = [index == iota + BF16(16 * i) for i in range(count // 16)]
    return jnp.concatenate(
        [jnp.where(m, part, zero) for v in values for part in two_parts(v) for m in masks], axis=0
    )


def product(rows, high_count, iota):
    left = jnp.concatenate(
        [weighted(as_bf16(high), values, high_count, iota) for high, _, values in rows], axis=1
    )
    right = jnp.concatenate([one_hot(as_bf16(low), LANES, iota) for _, low, _ in rows], axis=1)
    return lax.dot_general(left, right, (((1,), (1,)), ((), ())), preferred_element_type=F32)


def scatter(row_of, high_count, group, beside=None):
    iota = iota16()

    def body(g, acc):
        start = pl.multiple_of(g * group, group)
        acc = acc + product(
            [row_of((start, k), half) for k in range(group) for half in range(2)], high_count, iota
        )
        if beside is not None:
            beside(start)
        return acc

    acc = lax.fori_loop(0, PAIRS // group, body, jnp.zeros((2 * high_count, LANES), F32))
    return acc[:high_count] + acc[high_count:]


def lane_row(ref, row):
    return jnp.broadcast_to(ref[pl.ds(row, 1), :], (16, LANES))


def pair_row(ref, pair, half):
    start, k = pair
    view = ref.at[pl.ds(start, 8 * (k // 8 + 1)), half * LANES : (half + 1) * LANES]
    return jnp.broadcast_to(view[k : k + 1, :], (16, LANES))


def cell_split(cell):
    return ((cell >> 7) & 1) * 64 + (cell >> 8), cell & (LANES - 1)


def node_split(node):
    return node >> 7, node & (LANES - 1)


def to_block(table):
    return jnp.concatenate([table[:64], table[64:]], axis=1).reshape(8, 8, 256)


def every(ref, first, per_pair, start):
    return ref.at[pl.ds(start * per_pair + first, 8, stride=per_pair), :]


def pack_air(air_ref, cell_ref, own_ref, out_ref, per_pair, start, count):
    table = air_rows(air_ref)
    for k in range(0, count, 8):
        at = pl.ds(pl.multiple_of(start + k, 8), 8)
        for half in range(2):
            weight = every(own_ref, 4 + half, 6, start + k)[...]
            values = gather(table, cell_ref[at, half * LANES : (half + 1) * LANES])
            every(out_ref, half, per_pair, start + k)[...] = weight * values


def pack_nodes(warmth_ref, node_ref, out_ref, per_pair, start, count):
    table = [warmth_ref[j : j + 1, :] for j in range(warmth_ref.shape[0])]
    for k in range(0, count, 8):
        at = pl.ds(pl.multiple_of(start + k, 8), 8)
        for half in range(2):
            values = gather(table, node_ref[at, half * LANES : (half + 1) * LANES])
            every(out_ref, 2 + half, per_pair, start + k)[...] = values


def send_out(own_ref, targets, sems, per_pair, start, count):
    at = pl.ds(pl.multiple_of(start * per_pair, 8), count * per_pair)
    for k, target in enumerate(targets):
        pltpu.make_async_copy(own_ref.at[at, :], target.at[at, :], sems.at[k]).start()


def wait_out(own_ref, targets, sems):
    for k, target in enumerate(targets):
        pltpu.make_async_copy(own_ref, target, sems.at[k]).wait()


def pre_kernel(
    air_in, enthalpy_in, cell_in, contact_in, rows_in, node_in, packed_out, kept_out,
    air_ref, enthalpy_ref, cell_ref, contact_ref, rows_ref, node_ref, sems, out_sems,
    warmth_ref, own_ref,
):
    copies = [
        pltpu.make_async_copy(source, target, sems.at[k])
        for k, (source, target) in enumerate(
            [
                (rows_in, rows_ref), (contact_in, contact_ref), (air_in, air_ref),
                (cell_in, cell_ref), (enthalpy_in, enthalpy_ref), (node_in, node_ref),
            ]
        )
    ]
    for copy in copies:
        copy.start()
    for copy in copies:
        copy.wait()
    live = jnp.transpose(jnp.broadcast_to(rows_ref[...], (LANES, LANES)))
    for half in range(2):
        lanes = slice(half * LANES, (half + 1) * LANES)
        spot = lax.broadcasted_iota(I32, (PAIRS, LANES), 1) + half * LANES
        own_ref[pl.ds(4 + half, PAIRS, stride=6), :] = jnp.where(
            spot < live, contact_ref[:, lanes], 0.0
        )
    warmth_ref[...] = node_temp(enthalpy_ref[...])

    def body(g, carry):
        start = pl.multiple_of(g * 32, 32)
        pack_nodes(warmth_ref, node_ref, own_ref, 6, start, 32)
        pack_air(air_ref, cell_ref, own_ref, own_ref, 6, start, 32)
        send_out(own_ref, (packed_out, kept_out), out_sems, 6, start, 32)
        return carry

    lax.fori_loop(0, PAIRS // 32, body, 0)
    wait_out(own_ref, (packed_out, kept_out), out_sems)


def conduction(warmth, links_ref):
    rows = []
    for b in range(warmth.shape[0]):
        linked = take(warmth[b : b + 1], links_ref[b])
        rows.append(jnp.sum(linked, axis=0, keepdims=True))
    return jnp.concatenate(rows, axis=0) - 8.0 * warmth


def air_step(air, velocity, fluid, behind_halo, ahead_halo, left_halo, right_halo, source):
    behind = jnp.concatenate([behind_halo, air[:-1]], axis=0)
    ahead = jnp.concatenate([air[1:], ahead_halo], axis=0)
    row = lax.broadcasted_iota(I32, air.shape, 1)
    lane = lax.broadcasted_iota(I32, air.shape, 2)
    low = jnp.where(row == 0, left_halo, pltpu.roll(air, 1, 1))
    high = jnp.where(row == 7, right_halo, pltpu.roll(air, 7, 1))
    flat = air.reshape(64, 256)
    left = jnp.where(lane == 0, 0.0, pltpu.roll(flat, 1, 1).reshape(air.shape))
    right = jnp.where(lane == 255, 0.0, pltpu.roll(flat, 255, 1).reshape(air.shape))
    laplace = (ahead + behind) + (high + low) + (right + left) - 6.0 * air
    advect = jnp.maximum(velocity, 0.0) * (air - behind) + jnp.minimum(velocity, 0.0) * (
        ahead - air
    )
    return air + fluid.astype(F32) * DT_AIR * (laplace - advect + source)


def air_part(
    own_ref, received_ref, first_ref, per_pair, air_ref, velocity_ref, fluid_ref, cell_ref,
    edge_refs, air_out_ref, beside,
):
    def heat_row(pair, half):
        p = pair[0] + pair[1]
        base = p * per_pair + half
        heat = lane_row(first_ref, p * 6 + 4 + half) * lane_row(received_ref, base + 2)
        heat = heat - lane_row(own_ref, base)
        return cell_split(pair_row(cell_ref, pair, half)) + ([heat],)

    heat = scatter(heat_row, 128, 32, beside)
    edges = []
    for axis, refs in (("len", edge_refs[:2]), ("hgt", edge_refs[2:])):
        at = lax.axis_index(axis)
        for ref, last in zip(refs, (0, lax.axis_size(axis) - 1)):
            edges.append(jnp.where(at == last, 0.0, ref[...]))
    air_out_ref[...] = air_step(
        air_ref[...], velocity_ref[...], fluid_ref[...], *edges, to_block(heat)
    )


def node_part(own_ref, received_ref, first_ref, per_pair, enthalpy_ref, links_ref, node_ref):
    def node_row(pair, half):
        p = pair[0] + pair[1]
        base = p * per_pair + half
        heat = lane_row(first_ref, p * 6 + 4 + half) * lane_row(own_ref, base + 2)
        heat = lane_row(received_ref, base) - heat
        return node_split(pair_row(node_ref, pair, half)) + ([heat],)

    gained = scatter(node_row, 32, 32)
    enthalpy = enthalpy_ref[...]
    return enthalpy + DT_NODE * (conduction(node_temp(enthalpy), links_ref) + gained)


def mid_kernel(
    own_ref, first_ref, air_ref, velocity_ref, fluid_ref, enthalpy_ref, links_ref, cell_ref,
    node_ref, behind_ref, ahead_ref, left_ref, right_ref,
    air_out_ref, enthalpy_out_ref, next_ref, packed_out, warmth_ref, out_sems,
):
    enthalpy = node_part(own_ref, first_ref, first_ref, 6, enthalpy_ref, links_ref, node_ref)
    enthalpy_out_ref[...] = enthalpy
    warmth_ref[...] = node_temp(enthalpy)
    air_part(
        own_ref, first_ref, own_ref, 6, air_ref, velocity_ref, fluid_ref, cell_ref,
        (behind_ref, ahead_ref, left_ref, right_ref), air_out_ref,
        lambda start: pack_nodes(warmth_ref, node_ref, next_ref, 4, start, 32),
    )

    def body(g, carry):
        start = pl.multiple_of(g * 32, 32)
        pack_air(air_out_ref, cell_ref, own_ref, next_ref, 4, start, 32)
        send_out(next_ref, (packed_out,), out_sems, 4, start, 32)
        return carry

    lax.fori_loop(0, PAIRS // 32, body, 0)
    wait_out(next_ref, (packed_out,), out_sems)


def post_kernel(
    kept_ref, own_ref, received_ref, first_ref, air_ref, velocity_ref, fluid_ref, enthalpy_ref,
    links_ref, cell_ref, node_ref, behind_ref, ahead_ref, left_ref, right_ref,
    air_out_ref, enthalpy_out_ref,
):
    enthalpy_out_ref[...] = node_part(
        own_ref, received_ref, first_ref, 4, enthalpy_ref, links_ref, node_ref
    )
    air_part(
        own_ref, received_ref, kept_ref, 4, air_ref, velocity_ref, fluid_ref, cell_ref,
        (behind_ref, ahead_ref, left_ref, right_ref), air_out_ref, None,
    )


VMEM = pl.BlockSpec(memory_space=pltpu.VMEM)
HBM = pl.BlockSpec(memory_space=pltpu.HBM)


def call(kernel, name, shapes, mebibytes, **options):
    return pl.pallas_call(
        kernel,
        out_shape=[jax.ShapeDtypeStruct(s, F32) for s in shapes],
        name=name,
        compiler_params=pltpu.CompilerParams(vmem_limit_bytes=mebibytes * 1024 * 1024),
        **options,
    )


def halos(air):
    out = []
    for axis, dim in (("len", 0), ("hgt", 1)):
        count = lax.axis_size(axis)
        ring = [(i, (i + 1) % count) for i in range(count)]
        head = lax.slice_in_dim(air, 0, 1, axis=dim)
        tail = lax.slice_in_dim(air, air.shape[dim] - 1, air.shape[dim], axis=dim)
        out.append(lax.ppermute(tail, axis, ring))
        out.append(lax.ppermute(head, axis, [(j, i) for i, j in ring]))
    return out


def exchange(packed):
    both = packed.reshape(PAIRS, 1, -1)
    both = lax.all_to_all(both, ("len", "hgt"), split_axis=0, concat_axis=0, tiled=True)
    return both.reshape(packed.shape)


def local(
    air_temp, velocity, fluid, enthalpy, adjacency_lists, send_cells, contact, pair_rows, recv_nodes
):
    cells, nodes = send_cells[0], recv_nodes[0]
    block, panel = air_temp.shape, enthalpy.shape
    arrays = (air_temp, enthalpy, cells, contact[0], pair_rows, nodes)
    wide, narrow = (6 * PAIRS, LANES), (4 * PAIRS, LANES)
    packed, kept = call(
        pre_kernel,
        "pack_first",
        [wide, wide],
        60,
        in_specs=[HBM] * len(arrays),
        out_specs=[HBM, HBM],
        scratch_shapes=[pltpu.VMEM(x.shape, x.dtype) for x in arrays]
        + [pltpu.SemaphoreType.DMA((len(arrays),)), pltpu.SemaphoreType.DMA((2,))]
        + [pltpu.VMEM(panel, F32), pltpu.VMEM(wide, F32)],
    )(*arrays)
    first = exchange(packed)
    edges = halos(air_temp)
    air, heat, own, packed = call(
        mid_kernel,
        "first_step",
        [block, panel, narrow, narrow],
        32,
        out_specs=[VMEM, VMEM, VMEM, HBM],
        scratch_shapes=[pltpu.VMEM(panel, F32), pltpu.SemaphoreType.DMA((1,))],
    )(
        kept, first, air_temp, velocity, fluid, enthalpy, adjacency_lists, cells, nodes, *edges
    )
    received = exchange(packed)
    edges = halos(air)
    air, heat = call(post_kernel, "second_step", [block, panel], 32)(
        kept, own, received, first, air, velocity, fluid, heat, adjacency_lists, cells, nodes,
        *edges,
    )
    return air, heat


def solution(mesh):
    rows = P(("len", "hgt"), None)
    lists = P(("len", "hgt"), None, None)
    grid = P("len", "hgt", None)
    in_specs = (grid, grid, grid, rows, lists, lists, lists, rows, lists)
    return jax.shard_map(
        local, mesh=mesh, in_specs=in_specs, out_specs=(grid, rows), check_vma=False
    )
```

```python
import jax
import jax.numpy as jnp
from jax import lax
from jax.experimental import pallas as pl
from jax.experimental.pallas import tpu as pltpu
from jax.sharding import PartitionSpec as P

LATENT = 1.0
SOLID_SLOPE = 2.0
DT_AIR = 0.1
DT_NODE = 0.05

F32 = jnp.float32
BF16 = jnp.bfloat16
I32 = jnp.int32
LANES = 128
PAIRS = 128
PAIR_ROWS = 256


def node_temp(enthalpy):
    return jnp.where(
        enthalpy < 0.0,
        SOLID_SLOPE * enthalpy,
        jnp.where(enthalpy > LATENT, enthalpy - LATENT, 0.0),
    )


def take(row, lane):
    return jnp.take_along_axis(jnp.broadcast_to(row, lane.shape), lane, axis=1)


def gather(rows, index):
    lane = index & (LANES - 1)
    bits = [((index >> (7 + b)) & 1) == 1 for b in range(len(rows).bit_length() - 1)]

    def pick(first, level):
        if level == 0:
            return take(rows[first], lane)
        low = pick(first, level - 1)
        high = pick(first + (1 << (level - 1)), level - 1)
        return jnp.where(bits[level - 1], high, low)

    return pick(0, len(bits))


def air_rows(air_ref):
    return [
        air_ref[i, j : j + 1, h : h + LANES]
        for i in range(8)
        for j in range(8)
        for h in (0, LANES)
    ]


def iota16():
    return lax.broadcasted_iota(I32, (16, LANES), 0).astype(F32).astype(BF16)


def as_bf16(index):
    return index.astype(F32).astype(BF16)


def two_parts(value):
    top = value.astype(BF16)
    return top, (value - top.astype(F32)).astype(BF16)


def one_hot(index, count, iota):
    one = jnp.ones((16, LANES), BF16)
    zero = jnp.zeros((16, LANES), BF16)
    return jnp.concatenate(
        [jnp.where(index == iota + BF16(16 * i), one, zero) for i in range(count // 16)], axis=0
    )


def weighted(index, values, count, iota):
    zero = jnp.zeros((16, LANES), BF16)
    masks = [index == iota + BF16(16 * i) for i in range(count // 16)]
    return jnp.concatenate(
        [jnp.where(m, part, zero) for v in values for part in two_parts(v) for m in masks], axis=0
    )


def product(rows, high_count, iota):
    left = jnp.concatenate(
        [weighted(as_bf16(high), values, high_count, iota) for high, _, values in rows], axis=1
    )
    right = jnp.concatenate([one_hot(as_bf16(low), LANES, iota) for _, low, _ in rows], axis=1)
    return lax.dot_general(left, right, (((1,), (1,)), ((), ())), preferred_element_type=F32)


def scatter(row_of, high_count, group, beside=None):
    iota = iota16()

    def body(g, acc):
        start = pl.multiple_of(g * group, group)
        acc = acc + product(
            [row_of((start, k), half) for k in range(group) for half in range(2)], high_count, iota
        )
        if beside is not None:
            beside(start)
        return acc

    acc = lax.fori_loop(0, PAIRS // group, body, jnp.zeros((2 * high_count, LANES), F32))
    return acc[:high_count] + acc[high_count:]


def lane_row(ref, row):
    return jnp.broadcast_to(ref[pl.ds(row, 1), :], (16, LANES))


def pair_row(ref, pair, half):
    start, k = pair
    view = ref.at[pl.ds(start, 8 * (k // 8 + 1)), half * LANES : (half + 1) * LANES]
    return jnp.broadcast_to(view[k : k + 1, :], (16, LANES))


def cell_split(cell):
    return ((cell >> 7) & 1) * 64 + (cell >> 8), cell & (LANES - 1)


def node_split(node):
    return node >> 7, node & (LANES - 1)


def to_block(table):
    return jnp.concatenate([table[:64], table[64:]], axis=1).reshape(8, 8, 256)


def every(ref, first, per_pair, start):
    return ref.at[pl.ds(start * per_pair + first, 8, stride=per_pair), :]


def turned(air_ref):
    flat = air_ref[...].reshape(64, 256)
    table = jnp.transpose(jnp.concatenate([flat[:, :LANES], flat[:, LANES:]], axis=0))
    return jnp.concatenate(two_parts(table), axis=1)


def gather_by_product(table, cells):
    iota = iota16()
    count = lax.broadcasted_iota(I32, (8, LANES), 0)
    hots, lows = [], []
    for cell in cells:
        for k in range(8):
            high, low = cell_split(jnp.broadcast_to(cell[k : k + 1], (16, LANES)))
            hots.append(one_hot(as_bf16(high), LANES, iota))
            lows.append(low[:8])
    hots = jnp.concatenate(hots, axis=1)
    found = lax.dot_general(
        table,
        jnp.concatenate([hots, hots], axis=0),
        (((1,), (0,)), ((), ())),
        preferred_element_type=F32,
    )
    rows = []
    for n, low in enumerate(lows):
        column = found[:, n * LANES : (n + 1) * LANES]
        level = [column[k : k + 8] for k in range(0, LANES, 8)]
        for b in range(3, 7):
            bit = ((low >> b) & 1) == 1
            level = [jnp.where(bit, y, x) for x, y in zip(level[::2], level[1::2])]
        rows.append(
            jnp.sum(jnp.where((low & 7) == count, level[0], 0.0), axis=0, keepdims=True)
        )
    return [jnp.concatenate(rows[k : k + 8], axis=0) for k in range(0, len(rows), 8)]


def pack_air(air_ref, turned_ref, cell_ref, own_ref, out_ref, per_pair, start, count, by_lane):
    table = air_rows(air_ref)
    blocks = [(k, half) for k in range(0, count, 8) for half in range(2)]
    cells = [
        cell_ref[pl.ds(pl.multiple_of(start + k, 8), 8), half * LANES : (half + 1) * LANES]
        for k, half in blocks
    ]
    found = gather_by_product(turned_ref[...], cells[by_lane:])
    found = [gather(table, cell) for cell in cells[:by_lane]] + found
    for (k, half), values in zip(blocks, found):
        weight = every(own_ref, 4 + half, 6, start + k)[...]
        every(out_ref, half, per_pair, start + k)[...] = weight * values


def pack_nodes(warmth_ref, node_ref, out_ref, per_pair, first, start, count):
    table = [warmth_ref[j : j + 1, :] for j in range(warmth_ref.shape[0])]
    for k in range(0, count, 8):
        at = pl.ds(pl.multiple_of(start + k, 8), 8)
        for half in range(2):
            values = gather(table, node_ref[at, half * LANES : (half + 1) * LANES])
            every(out_ref, first + half, per_pair, start + k)[...] = values


def send_out(own_ref, targets, sems, per_pair, start, count):
    at = pl.ds(pl.multiple_of(start * per_pair, 8), count * per_pair)
    for k, target in enumerate(targets):
        pltpu.make_async_copy(own_ref.at[at, :], target.at[at, :], sems.at[k]).start()


def wait_out(own_ref, targets, sems):
    for k, target in enumerate(targets):
        pltpu.make_async_copy(own_ref, target, sems.at[k]).wait()


def pre_kernel(
    air_in, enthalpy_in, cell_in, contact_in, rows_in, node_in, packed_out, kept_out,
    air_ref, enthalpy_ref, cell_ref, contact_ref, rows_ref, node_ref, sems, out_sems,
    warmth_ref, turned_ref, own_ref,
):
    copies = [
        pltpu.make_async_copy(source, target, sems.at[k])
        for k, (source, target) in enumerate(
            [
                (rows_in, rows_ref), (contact_in, contact_ref), (air_in, air_ref),
                (cell_in, cell_ref), (enthalpy_in, enthalpy_ref), (node_in, node_ref),
            ]
        )
    ]
    for copy in copies:
        copy.start()
    for copy in copies:
        copy.wait()
    live = jnp.transpose(jnp.broadcast_to(rows_ref[...], (LANES, LANES)))
    for half in range(2):
        lanes = slice(half * LANES, (half + 1) * LANES)
        spot = lax.broadcasted_iota(I32, (PAIRS, LANES), 1) + half * LANES
        own_ref[pl.ds(4 + half, PAIRS, stride=6), :] = jnp.where(
            spot < live, contact_ref[:, lanes], 0.0
        )
    warmth_ref[...] = node_temp(enthalpy_ref[...])
    turned_ref[...] = turned(air_ref)

    def body(g, carry):
        start = pl.multiple_of(g * 32, 32)
        pack_nodes(warmth_ref, node_ref, own_ref, 6, 2, start, 32)
        pack_air(air_ref, turned_ref, cell_ref, own_ref, own_ref, 6, start, 32, 2)
        send_out(own_ref, (packed_out, kept_out), out_sems, 6, start, 32)
        return carry

    lax.fori_loop(0, PAIRS // 32, body, 0)
    wait_out(own_ref, (packed_out, kept_out), out_sems)


def conduction(warmth, links_ref):
    rows = []
    for b in range(warmth.shape[0]):
        linked = take(warmth[b : b + 1], links_ref[b])
        rows.append(jnp.sum(linked, axis=0, keepdims=True))
    return jnp.concatenate(rows, axis=0) - 8.0 * warmth


def air_step(air, velocity, fluid, behind_halo, ahead_halo, left_halo, right_halo, source):
    behind = jnp.concatenate([behind_halo, air[:-1]], axis=0)
    ahead = jnp.concatenate([air[1:], ahead_halo], axis=0)
    row = lax.broadcasted_iota(I32, air.shape, 1)
    lane = lax.broadcasted_iota(I32, air.shape, 2)
    low = jnp.where(row == 0, left_halo, pltpu.roll(air, 1, 1))
    high = jnp.where(row == 7, right_halo, pltpu.roll(air, 7, 1))
    flat = air.reshape(64, 256)
    left = jnp.where(lane == 0, 0.0, pltpu.roll(flat, 1, 1).reshape(air.shape))
    right = jnp.where(lane == 255, 0.0, pltpu.roll(flat, 255, 1).reshape(air.shape))
    laplace = (ahead + behind) + (high + low) + (right + left) - 6.0 * air
    advect = jnp.maximum(velocity, 0.0) * (air - behind) + jnp.minimum(velocity, 0.0) * (
        ahead - air
    )
    return air + fluid.astype(F32) * DT_AIR * (laplace - advect + source)


def heat_part(own_ref, received_ref, first_ref, per_pair, cell_ref, heat_ref, beside=None):
    def heat_row(pair, half):
        p = pair[0] + pair[1]
        base = p * per_pair + half
        heat = lane_row(first_ref, p * 6 + 4 + half) * lane_row(received_ref, base + 2)
        heat = heat - lane_row(own_ref, base)
        return cell_split(pair_row(cell_ref, pair, half)) + ([heat],)

    heat_ref[...] = to_block(scatter(heat_row, 128, 32, beside))


def air_part(heat_ref, air_ref, velocity_ref, fluid_ref, edge_refs, air_out_ref):
    edges = []
    for axis, refs in (("len", edge_refs[:2]), ("hgt", edge_refs[2:])):
        at = lax.axis_index(axis)
        for ref, last in zip(refs, (0, lax.axis_size(axis) - 1)):
            edges.append(jnp.where(at == last, 0.0, ref[...]))
    air_out_ref[...] = air_step(
        air_ref[...], velocity_ref[...], fluid_ref[...], *edges, heat_ref[...]
    )


def node_part(own_ref, received_ref, first_ref, per_pair, enthalpy_ref, links_ref, node_ref):
    def node_row(pair, half):
        p = pair[0] + pair[1]
        base = p * per_pair + half
        heat = lane_row(first_ref, p * 6 + 4 + half) * lane_row(own_ref, base + 2)
        heat = lane_row(received_ref, base) - heat
        return node_split(pair_row(node_ref, pair, half)) + ([heat],)

    gained = scatter(node_row, 32, 32)
    enthalpy = enthalpy_ref[...]
    return enthalpy + DT_NODE * (conduction(node_temp(enthalpy), links_ref) + gained)


def mid_sums_kernel(
    own_ref, first_ref, enthalpy_ref, links_ref, cell_ref, node_ref,
    enthalpy_out_ref, heat_ref, surface_ref, warmth_ref,
):
    enthalpy = node_part(own_ref, first_ref, first_ref, 6, enthalpy_ref, links_ref, node_ref)
    enthalpy_out_ref[...] = enthalpy
    warmth_ref[...] = node_temp(enthalpy)
    heat_part(
        own_ref, first_ref, own_ref, 6, cell_ref, heat_ref,
        lambda start: pack_nodes(warmth_ref, node_ref, surface_ref, 2, 0, start, 32),
    )


def mid_air_kernel(
    own_ref, heat_ref, surface_ref, air_ref, velocity_ref, fluid_ref, cell_ref, behind_ref,
    ahead_ref, left_ref, right_ref, air_out_ref, next_ref, packed_out, turned_ref, out_sems,
):
    air_part(
        heat_ref, air_ref, velocity_ref, fluid_ref, (behind_ref, ahead_ref, left_ref, right_ref),
        air_out_ref,
    )
    turned_ref[...] = turned(air_out_ref)
    for half in range(2):
        next_ref[pl.ds(2 + half, PAIRS, stride=4), :] = surface_ref[pl.ds(half, PAIRS, stride=2), :]

    def body(g, carry):
        start = pl.multiple_of(g * 32, 32)
        pack_air(air_out_ref, turned_ref, cell_ref, own_ref, next_ref, 4, start, 32, 3)
        send_out(next_ref, (packed_out,), out_sems, 4, start, 32)
        return carry

    lax.fori_loop(0, PAIRS // 32, body, 0)
    wait_out(next_ref, (packed_out,), out_sems)


def post_sums_kernel(
    kept_ref, own_ref, received_ref, first_ref, enthalpy_ref, links_ref, cell_ref, node_ref,
    enthalpy_out_ref, heat_ref,
):
    enthalpy_out_ref[...] = node_part(
        own_ref, received_ref, first_ref, 4, enthalpy_ref, links_ref, node_ref
    )
    heat_part(own_ref, received_ref, kept_ref, 4, cell_ref, heat_ref)


def post_air_kernel(
    heat_ref, air_ref, velocity_ref, fluid_ref, behind_ref, ahead_ref, left_ref, right_ref,
    air_out_ref,
):
    air_part(
        heat_ref, air_ref, velocity_ref, fluid_ref, (behind_ref, ahead_ref, left_ref, right_ref),
        air_out_ref,
    )


VMEM = pl.BlockSpec(memory_space=pltpu.VMEM)
HBM = pl.BlockSpec(memory_space=pltpu.HBM)


def call(kernel, name, shapes, mebibytes, **options):
    return pl.pallas_call(
        kernel,
        out_shape=[jax.ShapeDtypeStruct(s, F32) for s in shapes],
        name=name,
        compiler_params=pltpu.CompilerParams(vmem_limit_bytes=mebibytes * 1024 * 1024),
        **options,
    )


def halos(air):
    out = []
    for axis, dim in (("len", 0), ("hgt", 1)):
        count = lax.axis_size(axis)
        ring = [(i, (i + 1) % count) for i in range(count)]
        head = lax.slice_in_dim(air, 0, 1, axis=dim)
        tail = lax.slice_in_dim(air, air.shape[dim] - 1, air.shape[dim], axis=dim)
        out.append(lax.ppermute(tail, axis, ring))
        out.append(lax.ppermute(head, axis, [(j, i) for i, j in ring]))
    return out


def exchange(packed):
    both = packed.reshape(PAIRS, 1, -1)
    both = lax.all_to_all(both, ("len", "hgt"), split_axis=0, concat_axis=0, tiled=True)
    return both.reshape(packed.shape)


def local(
    air_temp, velocity, fluid, enthalpy, adjacency_lists, send_cells, contact, pair_rows, recv_nodes
):
    cells, nodes = send_cells[0], recv_nodes[0]
    block, panel = air_temp.shape, enthalpy.shape
    arrays = (air_temp, enthalpy, cells, contact[0], pair_rows, nodes)
    wide, narrow = (6 * PAIRS, LANES), (4 * PAIRS, LANES)
    packed, kept = call(
        pre_kernel,
        "pack_first",
        [wide, wide],
        60,
        in_specs=[HBM] * len(arrays),
        out_specs=[HBM, HBM],
        scratch_shapes=[pltpu.VMEM(x.shape, x.dtype) for x in arrays]
        + [pltpu.SemaphoreType.DMA((len(arrays),)), pltpu.SemaphoreType.DMA((2,))]
        + [pltpu.VMEM(panel, F32), pltpu.VMEM((LANES, 2 * LANES), BF16), pltpu.VMEM(wide, F32)],
    )(*arrays)
    first = exchange(packed)
    edges = halos(air_temp)
    enthalpy, heat, surface = call(
        mid_sums_kernel,
        "first_sums",
        [panel, block, (2 * PAIRS, LANES)],
        32,
        scratch_shapes=[pltpu.VMEM(panel, F32)],
    )(kept, first, enthalpy, adjacency_lists, cells, nodes)
    air, own, packed = call(
        mid_air_kernel,
        "first_air",
        [block, narrow, narrow],
        32,
        out_specs=[VMEM, VMEM, HBM],
        scratch_shapes=[
            pltpu.VMEM((LANES, 2 * LANES), BF16),
            pltpu.SemaphoreType.DMA((1,)),
        ],
    )(kept, heat, surface, air_temp, velocity, fluid, cells, *edges)
    received = exchange(packed)
    edges = halos(air)
    enthalpy, heat = call(post_sums_kernel, "second_sums", [panel, block], 32)(
        kept, own, received, first, enthalpy, adjacency_lists, cells, nodes
    )
    (air,) = call(post_air_kernel, "second_air", [block], 32)(heat, air, velocity, fluid, *edges)
    return air, enthalpy


def solution(mesh):
    rows = P(("len", "hgt"), None)
    lists = P(("len", "hgt"), None, None)
    grid = P("len", "hgt", None)
    in_specs = (grid, grid, grid, rows, lists, lists, lists, rows, lists)
    return jax.shard_map(
        local, mesh=mesh, in_specs=in_specs, out_specs=(grid, rows), check_vma=False
    )
```

```python
import jax
import jax.numpy as jnp
from jax import lax
from jax.experimental import pallas as pl
from jax.experimental.pallas import tpu as pltpu
from jax.sharding import PartitionSpec as P

LATENT = 1.0
SOLID_SLOPE = 2.0
DT_AIR = 0.1
DT_NODE = 0.05

F32 = jnp.float32
BF16 = jnp.bfloat16
I32 = jnp.int32
LANES = 128
PAIRS = 128
PAIR_ROWS = 256


def node_temp(enthalpy):
    return jnp.where(
        enthalpy < 0.0,
        SOLID_SLOPE * enthalpy,
        jnp.where(enthalpy > LATENT, enthalpy - LATENT, 0.0),
    )


def take(row, lane):
    return jnp.take_along_axis(jnp.broadcast_to(row, lane.shape), lane, axis=1)


def gather(rows, index):
    lane = index & (LANES - 1)
    bits = [((index >> (7 + b)) & 1) == 1 for b in range(len(rows).bit_length() - 1)]

    def pick(first, level):
        if level == 0:
            return take(rows[first], lane)
        low = pick(first, level - 1)
        high = pick(first + (1 << (level - 1)), level - 1)
        return jnp.where(bits[level - 1], high, low)

    return pick(0, len(bits))


def air_rows(air_ref):
    return [
        air_ref[i, j : j + 1, h : h + LANES]
        for i in range(8)
        for j in range(8)
        for h in (0, LANES)
    ]


def iota16():
    return lax.broadcasted_iota(I32, (16, LANES), 0).astype(F32).astype(BF16)


def as_bf16(index):
    return index.astype(F32).astype(BF16)


def two_parts(value):
    top = value.astype(BF16)
    return top, (value - top.astype(F32)).astype(BF16)


def one_hot(index, count, iota):
    return one_hot_of(index, [iota + BF16(16 * i) for i in range(count // 16)])


def one_hot_of(index, marks):
    one = jnp.ones((16, LANES), BF16)
    zero = jnp.zeros((16, LANES), BF16)
    return jnp.concatenate([jnp.where(index == mark, one, zero) for mark in marks], axis=0)


def weighted(index, values, count, iota):
    zero = jnp.zeros((16, LANES), BF16)
    masks = [index == iota + BF16(16 * i) for i in range(count // 16)]
    return jnp.concatenate(
        [jnp.where(m, part, zero) for v in values for part in two_parts(v) for m in masks], axis=0
    )


def product(rows, high_count, low_count, iota):
    left = jnp.concatenate(
        [weighted(as_bf16(high), values, high_count, iota) for high, _, values in rows], axis=1
    )
    right = jnp.concatenate([one_hot(as_bf16(low), low_count, iota) for _, low, _ in rows], axis=1)
    return lax.dot_general(left, right, (((1,), (1,)), ((), ())), preferred_element_type=F32)


def scatter(row_of, split, beside=None, group=64):
    iota = iota16()
    high_count, low_count, digits = split

    def body(g, total):
        start = pl.multiple_of(g * group, group)
        for at in range(0, group, 8):
            rows = []
            for k in range(at, at + 8):
                for half in range(2):
                    index, value = row_of((start, k), half)
                    rows.append(digits(index) + ([value],))
            total = total + product(rows, high_count, low_count, iota)
        if beside is not None:
            beside(start, group)
        return total

    total = lax.fori_loop(0, PAIRS // group, body, jnp.zeros((2 * high_count, low_count), F32))
    return total[:high_count] + total[high_count:]


def lane_row(ref, row):
    return jnp.broadcast_to(ref[pl.ds(row, 1), :], (16, LANES))


def pair_row(ref, pair, half):
    start, k = pair
    view = ref.at[pl.ds(start, 8 * (k // 8 + 1)), half * LANES : (half + 1) * LANES]
    return jnp.broadcast_to(view[k : k + 1, :], (16, LANES))


def cell_split(cell):
    return ((cell >> 7) & 1) * 64 + (cell >> 8), cell & (LANES - 1)


CELL_SPLIT = (128, 128, cell_split)
NODE_SPLIT = (64, 64, lambda node: (((node >> 6) & 1) * 32 + (node >> 7), node & 63))


def to_block(table):
    return jnp.concatenate([table[:64], table[64:]], axis=1).reshape(8, 8, 256)


def every(ref, first, per_pair, start):
    return ref.at[pl.ds(start * per_pair + first, 8, stride=per_pair), :]


def turned(air_ref):
    flat = air_ref[...].reshape(64, 256)
    table = jnp.transpose(jnp.concatenate([flat[:, :LANES], flat[:, LANES:]], axis=0))
    return jnp.concatenate(two_parts(table), axis=1)


def gather_by_product(table, cells):
    iota = iota16()
    marks = [iota + iota + BF16(32 * i + half) for half in range(2) for i in range(4)]
    count = lax.broadcasted_iota(I32, (8, LANES), 0)
    hots, lows = [], []
    for cell in cells:
        for k in range(8):
            row = cell[k : k + 1]
            hots.append(one_hot_of(as_bf16(jnp.broadcast_to(row >> 7, (16, LANES))), marks))
            lows.append(jnp.broadcast_to(row, (8, LANES)))
    hots = jnp.concatenate(hots, axis=1)
    found = lax.dot_general(
        table,
        jnp.concatenate([hots, hots], axis=0),
        (((1,), (0,)), ((), ())),
        preferred_element_type=F32,
    )
    rows = []
    for n, low in enumerate(lows):
        column = found[:, n * LANES : (n + 1) * LANES]
        level = [column[k : k + 8] for k in range(0, LANES, 8)]
        for b in range(3, 7):
            bit = (low & (1 << b)) != 0
            level = [jnp.where(bit, y, x) for x, y in zip(level[::2], level[1::2])]
        rows.append(
            jnp.sum(jnp.where((low & 7) == count, level[0], 0.0), axis=0, keepdims=True)
        )
    return [jnp.concatenate(rows[k : k + 8], axis=0) for k in range(0, len(rows), 8)]


def pack_air(air_ref, turned_ref, cell_ref, own_ref, out_ref, per_pair, start, count, by_lane):
    table = air_rows(air_ref)
    blocks = [(k, half) for k in range(0, count, 8) for half in range(2)]
    cells = [
        cell_ref[pl.ds(pl.multiple_of(start + k, 8), 8), half * LANES : (half + 1) * LANES]
        for k, half in blocks
    ]
    found = gather_by_product(turned_ref[...], cells[by_lane:])
    found = [gather(table, cell) for cell in cells[:by_lane]] + found
    for (k, half), values in zip(blocks, found):
        weight = every(own_ref, 4 + half, 6, start + k)[...]
        every(out_ref, half, per_pair, start + k)[...] = weight * values


def pack_nodes(warmth_ref, node_ref, out_ref, per_pair, first, start, count):
    table = [warmth_ref[j : j + 1, :] for j in range(warmth_ref.shape[0])]
    for k in range(0, count, 8):
        at = pl.ds(pl.multiple_of(start + k, 8), 8)
        for half in range(2):
            values = gather(table, node_ref[at, half * LANES : (half + 1) * LANES])
            every(out_ref, first + half, per_pair, start + k)[...] = values


def send_out(own_ref, targets, sems, per_pair, start, count):
    at = pl.ds(pl.multiple_of(start * per_pair, 8), count * per_pair)
    for k, target in enumerate(targets):
        pltpu.make_async_copy(own_ref.at[at, :], target.at[at, :], sems.at[k]).start()


def wait_out(own_ref, targets, sems):
    for k, target in enumerate(targets):
        pltpu.make_async_copy(own_ref, target, sems.at[k]).wait()


def pre_kernel(
    air_in, enthalpy_in, cell_in, contact_in, rows_in, node_in, packed_out, kept_out,
    air_ref, enthalpy_ref, cell_ref, contact_ref, rows_ref, node_ref, sems, out_sems,
    warmth_ref, turned_ref, own_ref,
):
    copies = [
        pltpu.make_async_copy(source, target, sems.at[k])
        for k, (source, target) in enumerate(
            [
                (rows_in, rows_ref), (contact_in, contact_ref), (air_in, air_ref),
                (cell_in, cell_ref), (enthalpy_in, enthalpy_ref), (node_in, node_ref),
            ]
        )
    ]
    for copy in copies:
        copy.start()
    for copy in copies:
        copy.wait()
    live = jnp.transpose(jnp.broadcast_to(rows_ref[...], (LANES, LANES)))
    for half in range(2):
        lanes = slice(half * LANES, (half + 1) * LANES)
        spot = lax.broadcasted_iota(I32, (PAIRS, LANES), 1) + half * LANES
        own_ref[pl.ds(4 + half, PAIRS, stride=6), :] = jnp.where(
            spot < live, contact_ref[:, lanes], 0.0
        )
    warmth_ref[...] = node_temp(enthalpy_ref[...])
    turned_ref[...] = turned(air_ref)

    def body(g, carry):
        start = pl.multiple_of(g * 32, 32)
        pack_nodes(warmth_ref, node_ref, own_ref, 6, 2, start, 32)
        pack_air(air_ref, turned_ref, cell_ref, own_ref, own_ref, 6, start, 32, 2)
        send_out(own_ref, (packed_out, kept_out), out_sems, 6, start, 32)
        return carry

    lax.fori_loop(0, PAIRS // 32, body, 0)
    wait_out(own_ref, (packed_out, kept_out), out_sems)


def conduction(warmth, links_ref):
    rows = []
    for b in range(warmth.shape[0]):
        linked = take(warmth[b : b + 1], links_ref[b])
        rows.append(jnp.sum(linked, axis=0, keepdims=True))
    return jnp.concatenate(rows, axis=0) - 8.0 * warmth


def air_step(air, velocity, fluid, behind_halo, ahead_halo, left_halo, right_halo, source):
    behind = jnp.concatenate([behind_halo, air[:-1]], axis=0)
    ahead = jnp.concatenate([air[1:], ahead_halo], axis=0)
    row = lax.broadcasted_iota(I32, air.shape, 1)
    lane = lax.broadcasted_iota(I32, air.shape, 2)
    low = jnp.where(row == 0, left_halo, pltpu.roll(air, 1, 1))
    high = jnp.where(row == 7, right_halo, pltpu.roll(air, 7, 1))
    flat = air.reshape(64, 256)
    left = jnp.where(lane == 0, 0.0, pltpu.roll(flat, 1, 1).reshape(air.shape))
    right = jnp.where(lane == 255, 0.0, pltpu.roll(flat, 255, 1).reshape(air.shape))
    laplace = (ahead + behind) + (high + low) + (right + left) - 6.0 * air
    advect = jnp.maximum(velocity, 0.0) * (air - behind) + jnp.minimum(velocity, 0.0) * (
        ahead - air
    )
    return air + fluid.astype(F32) * DT_AIR * (laplace - advect + source)


def heat_part(own_ref, received_ref, first_ref, per_pair, cell_ref, heat_ref, beside=None):
    def heat_row(pair, half):
        p = pair[0] + pair[1]
        base = p * per_pair + half
        heat = lane_row(first_ref, p * 6 + 4 + half) * lane_row(received_ref, base + 2)
        heat = heat - lane_row(own_ref, base)
        return pair_row(cell_ref, pair, half), heat

    heat_ref[...] = to_block(scatter(heat_row, CELL_SPLIT, beside))


def air_part(heat_ref, air_ref, velocity_ref, fluid_ref, edge_refs, air_out_ref):
    edges = []
    for axis, refs in (("len", edge_refs[:2]), ("hgt", edge_refs[2:])):
        at = lax.axis_index(axis)
        for ref, last in zip(refs, (0, lax.axis_size(axis) - 1)):
            edges.append(jnp.where(at == last, 0.0, ref[...]))
    air_out_ref[...] = air_step(
        air_ref[...], velocity_ref[...], fluid_ref[...], *edges, heat_ref[...]
    )


def node_part(own_ref, received_ref, first_ref, per_pair, enthalpy_ref, links_ref, node_ref):
    def node_row(pair, half):
        p = pair[0] + pair[1]
        base = p * per_pair + half
        heat = lane_row(first_ref, p * 6 + 4 + half) * lane_row(own_ref, base + 2)
        heat = lane_row(received_ref, base) - heat
        return pair_row(node_ref, pair, half), heat

    gained = scatter(node_row, NODE_SPLIT)
    gained = jnp.concatenate([gained[:32], gained[32:]], axis=1)
    enthalpy = enthalpy_ref[...]
    return enthalpy + DT_NODE * (conduction(node_temp(enthalpy), links_ref) + gained)


def mid_sums_kernel(
    own_ref, first_ref, enthalpy_ref, links_ref, cell_ref, node_ref,
    enthalpy_out_ref, heat_ref, surface_ref, warmth_ref,
):
    enthalpy = node_part(own_ref, first_ref, first_ref, 6, enthalpy_ref, links_ref, node_ref)
    enthalpy_out_ref[...] = enthalpy
    warmth_ref[...] = node_temp(enthalpy)
    heat_part(
        own_ref, first_ref, own_ref, 6, cell_ref, heat_ref,
        lambda start, count: pack_nodes(
            warmth_ref, node_ref, surface_ref, 2, 0, start, count
        ),
    )


def mid_air_kernel(
    own_ref, heat_ref, surface_ref, air_ref, velocity_ref, fluid_ref, cell_ref, behind_ref,
    ahead_ref, left_ref, right_ref, air_out_ref, next_ref, packed_out, turned_ref, out_sems,
):
    air_part(
        heat_ref, air_ref, velocity_ref, fluid_ref, (behind_ref, ahead_ref, left_ref, right_ref),
        air_out_ref,
    )
    turned_ref[...] = turned(air_out_ref)
    for half in range(2):
        next_ref[pl.ds(2 + half, PAIRS, stride=4), :] = surface_ref[pl.ds(half, PAIRS, stride=2), :]

    def body(g, carry):
        start = pl.multiple_of(g * 32, 32)
        pack_air(air_out_ref, turned_ref, cell_ref, own_ref, next_ref, 4, start, 32, 3)
        send_out(next_ref, (packed_out,), out_sems, 4, start, 32)
        return carry

    lax.fori_loop(0, PAIRS // 32, body, 0)
    wait_out(next_ref, (packed_out,), out_sems)


def post_sums_kernel(
    kept_ref, own_ref, received_ref, first_ref, enthalpy_ref, links_ref, cell_ref, node_ref,
    enthalpy_out_ref, heat_ref,
):
    enthalpy_out_ref[...] = node_part(
        own_ref, received_ref, first_ref, 4, enthalpy_ref, links_ref, node_ref
    )
    heat_part(own_ref, received_ref, kept_ref, 4, cell_ref, heat_ref)


def post_air_kernel(
    heat_ref, air_ref, velocity_ref, fluid_ref, behind_ref, ahead_ref, left_ref, right_ref,
    air_out_ref,
):
    air_part(
        heat_ref, air_ref, velocity_ref, fluid_ref, (behind_ref, ahead_ref, left_ref, right_ref),
        air_out_ref,
    )


VMEM = pl.BlockSpec(memory_space=pltpu.VMEM)
HBM = pl.BlockSpec(memory_space=pltpu.HBM)


def call(kernel, name, shapes, mebibytes, **options):
    return pl.pallas_call(
        kernel,
        out_shape=[jax.ShapeDtypeStruct(s, F32) for s in shapes],
        name=name,
        compiler_params=pltpu.CompilerParams(vmem_limit_bytes=mebibytes * 1024 * 1024),
        **options,
    )


def halos(air):
    out = []
    for axis, dim in (("len", 0), ("hgt", 1)):
        count = lax.axis_size(axis)
        ring = [(i, (i + 1) % count) for i in range(count)]
        head = lax.slice_in_dim(air, 0, 1, axis=dim)
        tail = lax.slice_in_dim(air, air.shape[dim] - 1, air.shape[dim], axis=dim)
        out.append(lax.ppermute(tail, axis, ring))
        out.append(lax.ppermute(head, axis, [(j, i) for i, j in ring]))
    return out


def exchange(packed):
    both = packed.reshape(PAIRS, 1, -1)
    both = lax.all_to_all(both, ("len", "hgt"), split_axis=0, concat_axis=0, tiled=True)
    return both.reshape(packed.shape)


def local(
    air_temp, velocity, fluid, enthalpy, adjacency_lists, send_cells, contact, pair_rows, recv_nodes
):
    cells, nodes = send_cells[0], recv_nodes[0]
    block, panel = air_temp.shape, enthalpy.shape
    arrays = (air_temp, enthalpy, cells, contact[0], pair_rows, nodes)
    wide, narrow = (6 * PAIRS, LANES), (4 * PAIRS, LANES)
    packed, kept = call(
        pre_kernel,
        "pack_first",
        [wide, wide],
        60,
        in_specs=[HBM] * len(arrays),
        out_specs=[HBM, HBM],
        scratch_shapes=[pltpu.VMEM(x.shape, x.dtype) for x in arrays]
        + [pltpu.SemaphoreType.DMA((len(arrays),)), pltpu.SemaphoreType.DMA((2,))]
        + [pltpu.VMEM(panel, F32), pltpu.VMEM((LANES, 2 * LANES), BF16), pltpu.VMEM(wide, F32)],
    )(*arrays)
    first = exchange(packed)
    edges = halos(air_temp)
    enthalpy, heat, surface = call(
        mid_sums_kernel,
        "first_sums",
        [panel, block, (2 * PAIRS, LANES)],
        32,
        scratch_shapes=[pltpu.VMEM(panel, F32)],
    )(kept, first, enthalpy, adjacency_lists, cells, nodes)
    air, own, packed = call(
        mid_air_kernel,
        "first_air",
        [block, narrow, narrow],
        32,
        out_specs=[VMEM, VMEM, HBM],
        scratch_shapes=[
            pltpu.VMEM((LANES, 2 * LANES), BF16),
            pltpu.SemaphoreType.DMA((1,)),
        ],
    )(kept, heat, surface, air_temp, velocity, fluid, cells, *edges)
    received = exchange(packed)
    edges = halos(air)
    enthalpy, heat = call(post_sums_kernel, "second_sums", [panel, block], 32)(
        kept, own, received, first, enthalpy, adjacency_lists, cells, nodes
    )
    (air,) = call(post_air_kernel, "second_air", [block], 32)(heat, air, velocity, fluid, *edges)
    return air, enthalpy


def solution(mesh):
    rows = P(("len", "hgt"), None)
    lists = P(("len", "hgt"), None, None)
    grid = P("len", "hgt", None)
    in_specs = (grid, grid, grid, rows, lists, lists, lists, rows, lists)
    return jax.shard_map(
        local, mesh=mesh, in_specs=in_specs, out_specs=(grid, rows), check_vma=False
    )
```

```python
import jax
import jax.numpy as jnp
from jax import lax
from jax.experimental import pallas as pl
from jax.experimental.pallas import tpu as pltpu
from jax.sharding import PartitionSpec as P

LATENT = 1.0
SOLID_SLOPE = 2.0
DT_AIR = 0.1
DT_NODE = 0.05

F32 = jnp.float32
BF16 = jnp.bfloat16
I32 = jnp.int32
LANES = 128
PAIRS = 128
PAIR_ROWS = 256


def node_temp(enthalpy):
    return jnp.where(
        enthalpy < 0.0,
        SOLID_SLOPE * enthalpy,
        jnp.where(enthalpy > LATENT, enthalpy - LATENT, 0.0),
    )


def take(row, lane):
    return jnp.take_along_axis(jnp.broadcast_to(row, lane.shape), lane, axis=1)


def gather(rows, index):
    lane = index & (LANES - 1)
    bits = [((index >> (7 + b)) & 1) == 1 for b in range(len(rows).bit_length() - 1)]

    def pick(first, level):
        if level == 0:
            return take(rows[first], lane)
        low = pick(first, level - 1)
        high = pick(first + (1 << (level - 1)), level - 1)
        return jnp.where(bits[level - 1], high, low)

    return pick(0, len(bits))


def air_rows(air_ref):
    return [
        air_ref[i, j : j + 1, h : h + LANES]
        for i in range(8)
        for j in range(8)
        for h in (0, LANES)
    ]


def iota16():
    return lax.broadcasted_iota(I32, (16, LANES), 0).astype(F32).astype(BF16)


def as_bf16(index):
    return index.astype(F32).astype(BF16)


def two_parts(value):
    top = value.astype(BF16)
    return top, (value - top.astype(F32)).astype(BF16)


def one_hot(index, count, iota):
    return one_hot_of(index, [iota + BF16(16 * i) for i in range(count // 16)])


def one_hot_of(index, marks):
    one = jnp.ones((16, LANES), BF16)
    zero = jnp.zeros((16, LANES), BF16)
    return jnp.concatenate([jnp.where(index == mark, one, zero) for mark in marks], axis=0)


def weighted(index, values, count, iota):
    zero = jnp.zeros((16, LANES), BF16)
    masks = [index == iota + BF16(16 * i) for i in range(count // 16)]
    return jnp.concatenate(
        [jnp.where(m, part, zero) for v in values for part in two_parts(v) for m in masks], axis=0
    )


def product(rows, high_count, low_count, iota):
    left = jnp.concatenate(
        [weighted(as_bf16(high), values, high_count, iota) for high, _, values in rows], axis=1
    )
    right = jnp.concatenate([one_hot(as_bf16(low), low_count, iota) for _, low, _ in rows], axis=1)
    return lax.dot_general(left, right, (((1,), (1,)), ((), ())), preferred_element_type=F32)


def scatter(row_of, split, beside=None, group=128):
    iota = iota16()
    high_count, low_count, digits = split

    def body(g, total):
        start = pl.multiple_of(g * group, group)
        for at in range(0, group, 8):
            rows = []
            for k in range(at, at + 8):
                for half in range(2):
                    index, value = row_of((start, k), half)
                    rows.append(digits(index) + ([value],))
            total = total + product(rows, high_count, low_count, iota)
        if beside is not None:
            beside(start, group)
        return total

    total = lax.fori_loop(0, PAIRS // group, body, jnp.zeros((2 * high_count, low_count), F32))
    return total[:high_count] + total[high_count:]


def lane_row(ref, row):
    return jnp.broadcast_to(ref[pl.ds(row, 1), :], (16, LANES))


def pair_row(ref, pair, half):
    start, k = pair
    view = ref.at[pl.ds(start, 8 * (k // 8 + 1)), half * LANES : (half + 1) * LANES]
    return jnp.broadcast_to(view[k : k + 1, :], (16, LANES))


def cell_split(cell):
    return ((cell >> 7) & 1) * 64 + (cell >> 8), cell & (LANES - 1)


CELL_SPLIT = (128, 128, cell_split)
NODE_SPLIT = (64, 64, lambda node: (((node >> 6) & 1) * 32 + (node >> 7), node & 63))


def to_block(table):
    return jnp.concatenate([table[:64], table[64:]], axis=1).reshape(8, 8, 256)


def every(ref, first, per_pair, start):
    return ref.at[pl.ds(start * per_pair + first, 8, stride=per_pair), :]


def turned(air_ref):
    flat = air_ref[...].reshape(64, 256)
    table = jnp.transpose(jnp.concatenate([flat[:, :LANES], flat[:, LANES:]], axis=0))
    return jnp.concatenate(two_parts(table), axis=1)


def gather_by_product(table, cells):
    iota = iota16()
    marks = [iota + iota + BF16(32 * i + half) for half in range(2) for i in range(4)]
    count = lax.broadcasted_iota(I32, (8, LANES), 0)
    hots, lows = [], []
    for cell in cells:
        for k in range(8):
            row = cell[k : k + 1]
            hots.append(one_hot_of(as_bf16(jnp.broadcast_to(row >> 7, (16, LANES))), marks))
            lows.append(jnp.broadcast_to(row, (8, LANES)))
    hots = jnp.concatenate(hots, axis=1)
    found = lax.dot_general(
        table,
        jnp.concatenate([hots, hots], axis=0),
        (((1,), (0,)), ((), ())),
        preferred_element_type=F32,
    )
    rows = []
    for n, low in enumerate(lows):
        column = found[:, n * LANES : (n + 1) * LANES]
        level = [column[k : k + 8] for k in range(0, LANES, 8)]
        for b in range(3, 7):
            bit = (low & (1 << b)) != 0
            level = [jnp.where(bit, y, x) for x, y in zip(level[::2], level[1::2])]
        rows.append(
            jnp.sum(jnp.where((low & 7) == count, level[0], 0.0), axis=0, keepdims=True)
        )
    return [jnp.concatenate(rows[k : k + 8], axis=0) for k in range(0, len(rows), 8)]


def pack_air(air_ref, turned_ref, cell_ref, own_ref, out_ref, per_pair, start, count, by_lane):
    table = air_rows(air_ref)
    blocks = [(k, half) for k in range(0, count, 8) for half in range(2)]
    cells = [
        cell_ref[pl.ds(pl.multiple_of(start + k, 8), 8), half * LANES : (half + 1) * LANES]
        for k, half in blocks
    ]
    found = gather_by_product(turned_ref[...], cells[by_lane:])
    found = [gather(table, cell) for cell in cells[:by_lane]] + found
    for (k, half), values in zip(blocks, found):
        weight = every(own_ref, 4 + half, 6, start + k)[...]
        every(out_ref, half, per_pair, start + k)[...] = weight * values


def pack_nodes(warmth_ref, node_ref, out_ref, per_pair, first, start, count):
    table = [warmth_ref[j : j + 1, :] for j in range(warmth_ref.shape[0])]
    for k in range(0, count, 8):
        at = pl.ds(pl.multiple_of(start + k, 8), 8)
        for half in range(2):
            values = gather(table, node_ref[at, half * LANES : (half + 1) * LANES])
            every(out_ref, first + half, per_pair, start + k)[...] = values


def send_out(own_ref, targets, sems, per_pair, start, count):
    at = pl.ds(pl.multiple_of(start * per_pair, 8), count * per_pair)
    for k, target in enumerate(targets):
        pltpu.make_async_copy(own_ref.at[at, :], target.at[at, :], sems.at[k]).start()


def wait_out(own_ref, targets, sems):
    for k, target in enumerate(targets):
        pltpu.make_async_copy(own_ref, target, sems.at[k]).wait()


def pre_kernel(
    air_in, enthalpy_in, cell_in, contact_in, rows_in, node_in, packed_out, kept_out,
    air_ref, enthalpy_ref, cell_ref, contact_ref, rows_ref, node_ref, sems, out_sems,
    warmth_ref, turned_ref, own_ref,
):
    copies = [
        pltpu.make_async_copy(source, target, sems.at[k])
        for k, (source, target) in enumerate(
            [
                (rows_in, rows_ref), (contact_in, contact_ref), (air_in, air_ref),
                (cell_in, cell_ref), (enthalpy_in, enthalpy_ref), (node_in, node_ref),
            ]
        )
    ]
    for copy in copies:
        copy.start()
    for copy in copies:
        copy.wait()
    live = jnp.transpose(jnp.broadcast_to(rows_ref[...], (LANES, LANES)))
    for half in range(2):
        lanes = slice(half * LANES, (half + 1) * LANES)
        spot = lax.broadcasted_iota(I32, (PAIRS, LANES), 1) + half * LANES
        own_ref[pl.ds(4 + half, PAIRS, stride=6), :] = jnp.where(
            spot < live, contact_ref[:, lanes], 0.0
        )
    warmth_ref[...] = node_temp(enthalpy_ref[...])
    turned_ref[...] = turned(air_ref)

    def body(g, carry):
        start = pl.multiple_of(g * 32, 32)
        pack_nodes(warmth_ref, node_ref, own_ref, 6, 2, start, 32)
        pack_air(air_ref, turned_ref, cell_ref, own_ref, own_ref, 6, start, 32, 2)
        send_out(own_ref, (packed_out, kept_out), out_sems, 6, start, 32)
        return carry

    lax.fori_loop(0, PAIRS // 32, body, 0)
    wait_out(own_ref, (packed_out, kept_out), out_sems)


def conduct(warmth_ref, links_ref, conducted_ref, start, count):
    blocks = warmth_ref.shape[0] * count // PAIRS
    first = start // count * blocks
    for k in range(blocks):
        at = pl.ds(first + k, 1)
        warmth = warmth_ref[at, :]
        linked = take(warmth, links_ref[first + k])
        conducted_ref[at, :] = jnp.sum(linked, axis=0, keepdims=True) - 8.0 * warmth


def air_step(air, velocity, fluid, behind_halo, ahead_halo, left_halo, right_halo, source):
    behind = jnp.concatenate([behind_halo, air[:-1]], axis=0)
    ahead = jnp.concatenate([air[1:], ahead_halo], axis=0)
    row = lax.broadcasted_iota(I32, air.shape, 1)
    lane = lax.broadcasted_iota(I32, air.shape, 2)
    low = jnp.where(row == 0, left_halo, pltpu.roll(air, 1, 1))
    high = jnp.where(row == 7, right_halo, pltpu.roll(air, 7, 1))
    flat = air.reshape(64, 256)
    left = jnp.where(lane == 0, 0.0, pltpu.roll(flat, 1, 1).reshape(air.shape))
    right = jnp.where(lane == 255, 0.0, pltpu.roll(flat, 255, 1).reshape(air.shape))
    laplace = (ahead + behind) + (high + low) + (right + left) - 6.0 * air
    advect = jnp.maximum(velocity, 0.0) * (air - behind) + jnp.minimum(velocity, 0.0) * (
        ahead - air
    )
    return air + fluid.astype(F32) * DT_AIR * (laplace - advect + source)


def heat_part(own_ref, received_ref, first_ref, per_pair, cell_ref, heat_ref, beside=None):
    def heat_row(pair, half):
        p = pair[0] + pair[1]
        base = p * per_pair + half
        heat = lane_row(first_ref, p * 6 + 4 + half) * lane_row(received_ref, base + 2)
        heat = heat - lane_row(own_ref, base)
        return pair_row(cell_ref, pair, half), heat

    heat_ref[...] = to_block(scatter(heat_row, CELL_SPLIT, beside))


def air_part(heat_ref, air_ref, velocity_ref, fluid_ref, edge_refs, air_out_ref):
    edges = []
    for axis, refs in (("len", edge_refs[:2]), ("hgt", edge_refs[2:])):
        at = lax.axis_index(axis)
        for ref, last in zip(refs, (0, lax.axis_size(axis) - 1)):
            edges.append(jnp.where(at == last, 0.0, ref[...]))
    air_out_ref[...] = air_step(
        air_ref[...], velocity_ref[...], fluid_ref[...], *edges, heat_ref[...]
    )


def node_part(
    own_ref, received_ref, first_ref, per_pair, enthalpy_ref, links_ref, node_ref, warmth_ref,
    conducted_ref,
):
    def node_row(pair, half):
        p = pair[0] + pair[1]
        base = p * per_pair + half
        heat = lane_row(first_ref, p * 6 + 4 + half) * lane_row(own_ref, base + 2)
        heat = lane_row(received_ref, base) - heat
        return pair_row(node_ref, pair, half), heat

    enthalpy = enthalpy_ref[...]
    warmth_ref[...] = node_temp(enthalpy)
    gained = scatter(
        node_row,
        NODE_SPLIT,
        lambda start, count: conduct(warmth_ref, links_ref, conducted_ref, start, count),
    )
    gained = jnp.concatenate([gained[:32], gained[32:]], axis=1)
    return enthalpy + DT_NODE * (conducted_ref[...] + gained)


def mid_sums_kernel(
    own_ref, first_ref, enthalpy_ref, links_ref, cell_ref, node_ref,
    enthalpy_out_ref, heat_ref, surface_ref, warmth_ref, conducted_ref,
):
    enthalpy = node_part(
        own_ref, first_ref, first_ref, 6, enthalpy_ref, links_ref, node_ref, warmth_ref,
        conducted_ref,
    )
    enthalpy_out_ref[...] = enthalpy
    warmth_ref[...] = node_temp(enthalpy)
    heat_part(
        own_ref, first_ref, own_ref, 6, cell_ref, heat_ref,
        lambda start, count: pack_nodes(
            warmth_ref, node_ref, surface_ref, 2, 0, start, count
        ),
    )


def mid_air_kernel(
    own_ref, heat_ref, surface_ref, air_ref, velocity_ref, fluid_ref, cell_ref, behind_ref,
    ahead_ref, left_ref, right_ref, air_out_ref, next_ref, packed_out, turned_ref, out_sems,
):
    air_part(
        heat_ref, air_ref, velocity_ref, fluid_ref, (behind_ref, ahead_ref, left_ref, right_ref),
        air_out_ref,
    )
    turned_ref[...] = turned(air_out_ref)
    for half in range(2):
        next_ref[pl.ds(2 + half, PAIRS, stride=4), :] = surface_ref[pl.ds(half, PAIRS, stride=2), :]

    def body(g, carry):
        start = pl.multiple_of(g * 64, 64)
        pack_air(air_out_ref, turned_ref, cell_ref, own_ref, next_ref, 4, start, 64, 6)
        send_out(next_ref, (packed_out,), out_sems, 4, start, 64)
        return carry

    lax.fori_loop(0, PAIRS // 64, body, 0)
    wait_out(next_ref, (packed_out,), out_sems)


def post_sums_kernel(
    kept_ref, own_ref, received_ref, first_ref, enthalpy_ref, links_ref, cell_ref, node_ref,
    enthalpy_out, heat_ref, warmth_ref, conducted_ref, last_ref, sem,
):
    last_ref[...] = node_part(
        own_ref, received_ref, first_ref, 4, enthalpy_ref, links_ref, node_ref, warmth_ref,
        conducted_ref,
    )
    copy = pltpu.make_async_copy(last_ref, enthalpy_out, sem)
    copy.start()
    heat_part(own_ref, received_ref, kept_ref, 4, cell_ref, heat_ref)
    copy.wait()


def post_air_kernel(
    heat_ref, air_ref, velocity_ref, fluid_ref, behind_ref, ahead_ref, left_ref, right_ref,
    air_out_ref,
):
    air_part(
        heat_ref, air_ref, velocity_ref, fluid_ref, (behind_ref, ahead_ref, left_ref, right_ref),
        air_out_ref,
    )


VMEM = pl.BlockSpec(memory_space=pltpu.VMEM)
HBM = pl.BlockSpec(memory_space=pltpu.HBM)


def call(kernel, name, shapes, mebibytes, **options):
    return pl.pallas_call(
        kernel,
        out_shape=[jax.ShapeDtypeStruct(s, F32) for s in shapes],
        name=name,
        compiler_params=pltpu.CompilerParams(vmem_limit_bytes=mebibytes * 1024 * 1024),
        **options,
    )


def halos(air):
    out = []
    for axis, dim in (("len", 0), ("hgt", 1)):
        count = lax.axis_size(axis)
        ring = [(i, (i + 1) % count) for i in range(count)]
        head = lax.slice_in_dim(air, 0, 1, axis=dim)
        tail = lax.slice_in_dim(air, air.shape[dim] - 1, air.shape[dim], axis=dim)
        out.append(lax.ppermute(tail, axis, ring))
        out.append(lax.ppermute(head, axis, [(j, i) for i, j in ring]))
    return out


def exchange(packed):
    both = packed.reshape(PAIRS, 1, -1)
    both = lax.all_to_all(both, ("len", "hgt"), split_axis=0, concat_axis=0, tiled=True)
    return both.reshape(packed.shape)


def local(
    air_temp, velocity, fluid, enthalpy, adjacency_lists, send_cells, contact, pair_rows, recv_nodes
):
    cells, nodes = send_cells[0], recv_nodes[0]
    block, panel = air_temp.shape, enthalpy.shape
    arrays = (air_temp, enthalpy, cells, contact[0], pair_rows, nodes)
    wide, narrow = (6 * PAIRS, LANES), (4 * PAIRS, LANES)
    packed, kept = call(
        pre_kernel,
        "pack_first",
        [wide, wide],
        60,
        in_specs=[HBM] * len(arrays),
        out_specs=[HBM, HBM],
        scratch_shapes=[pltpu.VMEM(x.shape, x.dtype) for x in arrays]
        + [pltpu.SemaphoreType.DMA((len(arrays),)), pltpu.SemaphoreType.DMA((2,))]
        + [pltpu.VMEM(panel, F32), pltpu.VMEM((LANES, 2 * LANES), BF16), pltpu.VMEM(wide, F32)],
    )(*arrays)
    first = exchange(packed)
    edges = halos(air_temp)
    enthalpy, heat, surface = call(
        mid_sums_kernel,
        "first_sums",
        [panel, block, (2 * PAIRS, LANES)],
        32,
        scratch_shapes=[pltpu.VMEM(panel, F32)] * 2,
    )(kept, first, enthalpy, adjacency_lists, cells, nodes)
    air, own, packed = call(
        mid_air_kernel,
        "first_air",
        [block, narrow, narrow],
        32,
        out_specs=[VMEM, VMEM, HBM],
        scratch_shapes=[
            pltpu.VMEM((LANES, 2 * LANES), BF16),
            pltpu.SemaphoreType.DMA((1,)),
        ],
    )(kept, heat, surface, air_temp, velocity, fluid, cells, *edges)
    received = exchange(packed)
    edges = halos(air)
    enthalpy, heat = call(
        post_sums_kernel,
        "second_sums",
        [panel, block],
        32,
        out_specs=[HBM, VMEM],
        scratch_shapes=[pltpu.VMEM(panel, F32)] * 3 + [pltpu.SemaphoreType.DMA],
    )(
        kept, own, received, first, enthalpy, adjacency_lists, cells, nodes
    )
    (air,) = call(post_air_kernel, "second_air", [block], 32)(heat, air, velocity, fluid, *edges)
    return air, enthalpy


def solution(mesh):
    rows = P(("len", "hgt"), None)
    lists = P(("len", "hgt"), None, None)
    grid = P("len", "hgt", None)
    in_specs = (grid, grid, grid, rows, lists, lists, lists, rows, lists)
    return jax.shard_map(
        local, mesh=mesh, in_specs=in_specs, out_specs=(grid, rows), check_vma=False
    )
```

```python
import jax
import jax.numpy as jnp
from jax import lax
from jax.experimental import pallas as pl
from jax.experimental.pallas import tpu as pltpu
from jax.sharding import PartitionSpec as P

LATENT = 1.0
SOLID_SLOPE = 2.0
DT_AIR = 0.1
DT_NODE = 0.05

F32 = jnp.float32
BF16 = jnp.bfloat16
I32 = jnp.int32
LANES = 128
PAIRS = 128
PAIR_ROWS = 256


def node_temp(enthalpy):
    return jnp.where(
        enthalpy < 0.0,
        SOLID_SLOPE * enthalpy,
        jnp.where(enthalpy > LATENT, enthalpy - LATENT, 0.0),
    )


def take(row, lane):
    return jnp.take_along_axis(jnp.broadcast_to(row, lane.shape), lane, axis=1)


def gather(rows, index):
    lane = index & (LANES - 1)
    bits = [((index >> (7 + b)) & 1) == 1 for b in range(len(rows).bit_length() - 1)]

    def pick(first, level):
        if level == 0:
            return take(rows[first], lane)
        low = pick(first, level - 1)
        high = pick(first + (1 << (level - 1)), level - 1)
        return jnp.where(bits[level - 1], high, low)

    return pick(0, len(bits))


def air_rows(air_ref):
    return [
        air_ref[i, j : j + 1, h : h + LANES]
        for i in range(8)
        for j in range(8)
        for h in (0, LANES)
    ]


def iota16():
    return lax.broadcasted_iota(I32, (16, LANES), 0).astype(F32).astype(BF16)


def as_bf16(index):
    return index.astype(F32).astype(BF16)


def two_parts(value):
    top = value.astype(BF16)
    return top, (value - top.astype(F32)).astype(BF16)


def one_hot(index, count, iota):
    return one_hot_of(index, [iota + BF16(16 * i) for i in range(count // 16)])


def one_hot_of(index, marks):
    one = jnp.ones((16, LANES), BF16)
    zero = jnp.zeros((16, LANES), BF16)
    return jnp.concatenate([jnp.where(index == mark, one, zero) for mark in marks], axis=0)


def weighted(index, values, count, iota):
    zero = jnp.zeros((16, LANES), BF16)
    masks = [index == iota + BF16(16 * i) for i in range(count // 16)]
    return jnp.concatenate(
        [jnp.where(m, part, zero) for v in values for part in two_parts(v) for m in masks], axis=0
    )


def product(rows, high_count, low_count, iota):
    left = jnp.concatenate(
        [weighted(as_bf16(high), values, high_count, iota) for high, _, values in rows], axis=1
    )
    right = jnp.concatenate([one_hot(as_bf16(low), low_count, iota) for _, low, _ in rows], axis=1)
    return lax.dot_general(left, right, (((1,), (1,)), ((), ())), preferred_element_type=F32)


def scatter(row_of, split, beside=None, group=128):
    iota = iota16()
    high_count, low_count, digits = split

    def body(g, total):
        start = pl.multiple_of(g * group, group)
        for at in range(0, group, 8):
            rows = []
            for k in range(at, at + 8):
                for half in range(2):
                    index, value = row_of((start, k), half)
                    rows.append(digits(index) + ([value],))
            total = total + product(rows, high_count, low_count, iota)
        if beside is not None:
            beside(start, group)
        return total

    total = lax.fori_loop(0, PAIRS // group, body, jnp.zeros((2 * high_count, low_count), F32))
    return total[:high_count] + total[high_count:]


def lane_row(ref, row):
    return jnp.broadcast_to(ref[pl.ds(row, 1), :], (16, LANES))


def pair_row(ref, pair, half):
    start, k = pair
    view = ref.at[pl.ds(start, 8 * (k // 8 + 1)), half * LANES : (half + 1) * LANES]
    return jnp.broadcast_to(view[k : k + 1, :], (16, LANES))


def cell_split(cell):
    return ((cell >> 7) & 1) * 64 + (cell >> 8), cell & (LANES - 1)


CELL_SPLIT = (128, 128, cell_split)
NODE_SPLIT = (64, 64, lambda node: (((node >> 6) & 1) * 32 + (node >> 7), node & 63))


def to_block(table):
    return jnp.concatenate([table[:64], table[64:]], axis=1).reshape(8, 8, 256)


def every(ref, first, per_pair, start):
    return ref.at[pl.ds(start * per_pair + first, 8, stride=per_pair), :]


def turned(air_ref):
    flat = air_ref[...].reshape(64, 256)
    table = jnp.transpose(jnp.concatenate([flat[:, :LANES], flat[:, LANES:]], axis=0))
    return jnp.concatenate(two_parts(table), axis=1)


def gather_by_product(table, cells):
    iota = iota16()
    marks = [iota + iota + BF16(32 * i + half) for half in range(2) for i in range(4)]
    count = lax.broadcasted_iota(I32, (8, LANES), 0)
    hots, lows = [], []
    for cell in cells:
        for k in range(8):
            row = cell[k : k + 1]
            hots.append(one_hot_of(as_bf16(jnp.broadcast_to(row >> 7, (16, LANES))), marks))
            lows.append(jnp.broadcast_to(row, (8, LANES)))
    hots = jnp.concatenate(hots, axis=1)
    found = lax.dot_general(
        table,
        jnp.concatenate([hots, hots], axis=0),
        (((1,), (0,)), ((), ())),
        preferred_element_type=F32,
    )
    rows = []
    for n, low in enumerate(lows):
        column = found[:, n * LANES : (n + 1) * LANES]
        level = [column[k : k + 8] for k in range(0, LANES, 8)]
        for b in range(3, 7):
            bit = (low & (1 << b)) != 0
            level = [jnp.where(bit, y, x) for x, y in zip(level[::2], level[1::2])]
        rows.append(
            jnp.sum(jnp.where((low & 7) == count, level[0], 0.0), axis=0, keepdims=True)
        )
    return [jnp.concatenate(rows[k : k + 8], axis=0) for k in range(0, len(rows), 8)]


def pack_air(air_ref, turned_ref, cell_ref, own_ref, out_ref, per_pair, start, count, by_lane):
    table = air_rows(air_ref)
    blocks = [(k, half) for k in range(0, count, 8) for half in range(2)]
    cells = [
        cell_ref[pl.ds(pl.multiple_of(start + k, 8), 8), half * LANES : (half + 1) * LANES]
        for k, half in blocks
    ]
    found = gather_by_product(turned_ref[...], cells[by_lane:])
    found = [gather(table, cell) for cell in cells[:by_lane]] + found
    for (k, half), values in zip(blocks, found):
        weight = every(own_ref, 4 + half, 6, start + k)[...]
        every(out_ref, half, per_pair, start + k)[...] = weight * values


def pack_nodes(warmth_ref, node_ref, out_ref, per_pair, first, start, count):
    table = [warmth_ref[j : j + 1, :] for j in range(warmth_ref.shape[0])]
    for k in range(0, count, 8):
        at = pl.ds(pl.multiple_of(start + k, 8), 8)
        for half in range(2):
            values = gather(table, node_ref[at, half * LANES : (half + 1) * LANES])
            every(out_ref, first + half, per_pair, start + k)[...] = values


def send_out(own_ref, targets, sems, per_pair, start, count):
    at = pl.ds(pl.multiple_of(start * per_pair, 8), count * per_pair)
    for k, target in enumerate(targets):
        pltpu.make_async_copy(own_ref.at[at, :], target.at[at, :], sems.at[k]).start()


def wait_out(own_ref, targets, sems):
    for k, target in enumerate(targets):
        pltpu.make_async_copy(own_ref, target, sems.at[k]).wait()


def pre_kernel(
    air_in, enthalpy_in, cell_in, contact_in, rows_in, node_in, packed_out, kept_out,
    air_ref, enthalpy_ref, cell_ref, contact_ref, rows_ref, node_ref, sems, out_sems,
    warmth_ref, turned_ref, own_ref,
):
    copies = [
        pltpu.make_async_copy(source, target, sems.at[k])
        for k, (source, target) in enumerate(
            [
                (rows_in, rows_ref), (contact_in, contact_ref), (air_in, air_ref),
                (cell_in, cell_ref), (enthalpy_in, enthalpy_ref), (node_in, node_ref),
            ]
        )
    ]
    for copy in copies:
        copy.start()
    for copy in copies:
        copy.wait()
    live = jnp.transpose(jnp.broadcast_to(rows_ref[...], (LANES, LANES)))
    for half in range(2):
        lanes = slice(half * LANES, (half + 1) * LANES)
        spot = lax.broadcasted_iota(I32, (PAIRS, LANES), 1) + half * LANES
        own_ref[pl.ds(4 + half, PAIRS, stride=6), :] = jnp.where(
            spot < live, contact_ref[:, lanes], 0.0
        )
    warmth_ref[...] = node_temp(enthalpy_ref[...])
    turned_ref[...] = turned(air_ref)

    def body(g, carry):
        start = pl.multiple_of(g * 32, 32)
        pack_nodes(warmth_ref, node_ref, own_ref, 6, 2, start, 32)
        pack_air(air_ref, turned_ref, cell_ref, own_ref, own_ref, 6, start, 32, 2)
        send_out(own_ref, (packed_out, kept_out), out_sems, 6, start, 32)
        return carry

    lax.fori_loop(0, PAIRS // 32, body, 0)
    wait_out(own_ref, (packed_out, kept_out), out_sems)


def conduct(warmth_ref, links_ref, conducted_ref, start, count):
    blocks = warmth_ref.shape[0] * count // PAIRS
    first = start // count * blocks
    for k in range(blocks):
        at = pl.ds(first + k, 1)
        warmth = warmth_ref[at, :]
        linked = take(warmth, links_ref[first + k])
        conducted_ref[at, :] = jnp.sum(linked, axis=0, keepdims=True) - 8.0 * warmth


def air_step(air, velocity, fluid, behind_halo, ahead_halo, left_halo, right_halo, source):
    behind = jnp.concatenate([behind_halo, air[:-1]], axis=0)
    ahead = jnp.concatenate([air[1:], ahead_halo], axis=0)
    row = lax.broadcasted_iota(I32, air.shape, 1)
    lane = lax.broadcasted_iota(I32, air.shape, 2)
    low = jnp.where(row == 0, left_halo, pltpu.roll(air, 1, 1))
    high = jnp.where(row == 7, right_halo, pltpu.roll(air, 7, 1))
    flat = air.reshape(64, 256)
    left = jnp.where(lane == 0, 0.0, pltpu.roll(flat, 1, 1).reshape(air.shape))
    right = jnp.where(lane == 255, 0.0, pltpu.roll(flat, 255, 1).reshape(air.shape))
    laplace = (ahead + behind) + (high + low) + (right + left) - 6.0 * air
    advect = jnp.maximum(velocity, 0.0) * (air - behind) + jnp.minimum(velocity, 0.0) * (
        ahead - air
    )
    return air + fluid.astype(F32) * DT_AIR * (laplace - advect + source)


def heat_part(own_ref, received_ref, first_ref, per_pair, cell_ref, heat_ref, beside=None):
    def heat_row(pair, half):
        p = pair[0] + pair[1]
        base = p * per_pair + half
        heat = lane_row(first_ref, p * 6 + 4 + half) * lane_row(received_ref, base + 2)
        heat = heat - lane_row(own_ref, base)
        return pair_row(cell_ref, pair, half), heat

    heat_ref[...] = to_block(scatter(heat_row, CELL_SPLIT, beside))


def air_part(heat_ref, air_ref, velocity_ref, fluid_ref, edge_refs, air_out_ref):
    edges = []
    for axis, refs in (("len", edge_refs[:2]), ("hgt", edge_refs[2:])):
        at = lax.axis_index(axis)
        for ref, last in zip(refs, (0, lax.axis_size(axis) - 1)):
            edges.append(jnp.where(at == last, 0.0, ref[...]))
    air_out_ref[...] = air_step(
        air_ref[...], velocity_ref[...], fluid_ref[...], *edges, heat_ref[...]
    )


def node_part(
    own_ref, received_ref, first_ref, per_pair, enthalpy_ref, links_ref, node_ref, warmth_ref,
    conducted_ref,
):
    def node_row(pair, half):
        p = pair[0] + pair[1]
        base = p * per_pair + half
        heat = lane_row(first_ref, p * 6 + 4 + half) * lane_row(own_ref, base + 2)
        heat = lane_row(received_ref, base) - heat
        return pair_row(node_ref, pair, half), heat

    enthalpy = enthalpy_ref[...]
    warmth_ref[...] = node_temp(enthalpy)
    gained = scatter(
        node_row,
        NODE_SPLIT,
        lambda start, count: conduct(warmth_ref, links_ref, conducted_ref, start, count),
    )
    gained = jnp.concatenate([gained[:32], gained[32:]], axis=1)
    return enthalpy + DT_NODE * (conducted_ref[...] + gained)


def mid_sums_kernel(
    own_ref, first_ref, enthalpy_ref, links_ref, cell_ref, node_ref,
    enthalpy_out_ref, heat_ref, surface_ref, warmth_ref, conducted_ref,
):
    enthalpy = node_part(
        own_ref, first_ref, first_ref, 6, enthalpy_ref, links_ref, node_ref, warmth_ref,
        conducted_ref,
    )
    enthalpy_out_ref[...] = enthalpy
    warmth_ref[...] = node_temp(enthalpy)
    heat_part(
        own_ref, first_ref, own_ref, 6, cell_ref, heat_ref,
        lambda start, count: pack_nodes(
            warmth_ref, node_ref, surface_ref, 2, 0, start, count
        ),
    )


def mid_air_kernel(
    own_ref, heat_ref, surface_ref, air_ref, velocity_ref, fluid_ref, cell_ref, behind_ref,
    ahead_ref, left_ref, right_ref, air_out_ref, next_ref, packed_out, turned_ref, out_sems,
):
    air_part(
        heat_ref, air_ref, velocity_ref, fluid_ref, (behind_ref, ahead_ref, left_ref, right_ref),
        air_out_ref,
    )
    turned_ref[...] = turned(air_out_ref)
    for half in range(2):
        next_ref[pl.ds(2 + half, PAIRS, stride=4), :] = surface_ref[pl.ds(half, PAIRS, stride=2), :]

    def body(g, carry):
        start = pl.multiple_of(g * 64, 64)
        pack_air(air_out_ref, turned_ref, cell_ref, own_ref, next_ref, 4, start, 64, 6)
        send_out(next_ref, (packed_out,), out_sems, 4, start, 64)
        return carry

    lax.fori_loop(0, PAIRS // 64, body, 0)
    wait_out(next_ref, (packed_out,), out_sems)


def post_kernel(
    kept_ref, own_ref, received_ref, first_ref, enthalpy_ref, links_ref, cell_ref, node_ref,
    air_ref, velocity_ref, fluid_ref, behind_ref, ahead_ref, left_ref, right_ref,
    air_out, enthalpy_out, heat_ref, warmth_ref, conducted_ref, last_ref, last_air_ref, sems,
):
    heat_part(own_ref, received_ref, kept_ref, 4, cell_ref, heat_ref)
    air_part(
        heat_ref, air_ref, velocity_ref, fluid_ref, (behind_ref, ahead_ref, left_ref, right_ref),
        last_air_ref,
    )
    air_copy = pltpu.make_async_copy(last_air_ref, air_out, sems.at[0])
    air_copy.start()
    last_ref[...] = node_part(
        own_ref, received_ref, first_ref, 4, enthalpy_ref, links_ref, node_ref, warmth_ref,
        conducted_ref,
    )
    copy = pltpu.make_async_copy(last_ref, enthalpy_out, sems.at[1])
    copy.start()
    air_copy.wait()
    copy.wait()


VMEM = pl.BlockSpec(memory_space=pltpu.VMEM)
HBM = pl.BlockSpec(memory_space=pltpu.HBM)


def call(kernel, name, shapes, mebibytes, **options):
    return pl.pallas_call(
        kernel,
        out_shape=[jax.ShapeDtypeStruct(s, F32) for s in shapes],
        name=name,
        compiler_params=pltpu.CompilerParams(vmem_limit_bytes=mebibytes * 1024 * 1024),
        **options,
    )


def halos(air):
    out = []
    for axis, dim in (("len", 0), ("hgt", 1)):
        count = lax.axis_size(axis)
        ring = [(i, (i + 1) % count) for i in range(count)]
        head = lax.slice_in_dim(air, 0, 1, axis=dim)
        tail = lax.slice_in_dim(air, air.shape[dim] - 1, air.shape[dim], axis=dim)
        out.append(lax.ppermute(tail, axis, ring))
        out.append(lax.ppermute(head, axis, [(j, i) for i, j in ring]))
    return out


def exchange(packed):
    both = packed.reshape(PAIRS, 1, -1)
    both = lax.all_to_all(both, ("len", "hgt"), split_axis=0, concat_axis=0, tiled=True)
    return both.reshape(packed.shape)


def local(
    air_temp, velocity, fluid, enthalpy, adjacency_lists, send_cells, contact, pair_rows, recv_nodes
):
    cells, nodes = send_cells[0], recv_nodes[0]
    block, panel = air_temp.shape, enthalpy.shape
    arrays = (air_temp, enthalpy, cells, contact[0], pair_rows, nodes)
    wide, narrow = (6 * PAIRS, LANES), (4 * PAIRS, LANES)
    packed, kept = call(
        pre_kernel,
        "pack_first",
        [wide, wide],
        60,
        in_specs=[HBM] * len(arrays),
        out_specs=[HBM, HBM],
        scratch_shapes=[pltpu.VMEM(x.shape, x.dtype) for x in arrays]
        + [pltpu.SemaphoreType.DMA((len(arrays),)), pltpu.SemaphoreType.DMA((2,))]
        + [pltpu.VMEM(panel, F32), pltpu.VMEM((LANES, 2 * LANES), BF16), pltpu.VMEM(wide, F32)],
    )(*arrays)
    first = exchange(packed)
    edges = halos(air_temp)
    enthalpy, heat, surface = call(
        mid_sums_kernel,
        "first_sums",
        [panel, block, (2 * PAIRS, LANES)],
        32,
        scratch_shapes=[pltpu.VMEM(panel, F32)] * 2,
    )(kept, first, enthalpy, adjacency_lists, cells, nodes)
    air, own, packed = call(
        mid_air_kernel,
        "first_air",
        [block, narrow, narrow],
        32,
        out_specs=[VMEM, VMEM, HBM],
        scratch_shapes=[
            pltpu.VMEM((LANES, 2 * LANES), BF16),
            pltpu.SemaphoreType.DMA((1,)),
        ],
    )(kept, heat, surface, air_temp, velocity, fluid, cells, *edges)
    received = exchange(packed)
    edges = halos(air)
    air, enthalpy = call(
        post_kernel,
        "second_step",
        [block, panel],
        32,
        out_specs=[HBM, HBM],
        scratch_shapes=[pltpu.VMEM(block, F32)]
        + [pltpu.VMEM(panel, F32)] * 3
        + [pltpu.VMEM(block, F32), pltpu.SemaphoreType.DMA((2,))],
    )(
        kept, own, received, first, enthalpy, adjacency_lists, cells, nodes, air, velocity, fluid,
        *edges,
    )
    return air, enthalpy


def solution(mesh):
    rows = P(("len", "hgt"), None)
    lists = P(("len", "hgt"), None, None)
    grid = P("len", "hgt", None)
    in_specs = (grid, grid, grid, rows, lists, lists, lists, rows, lists)
    return jax.shard_map(
        local, mesh=mesh, in_specs=in_specs, out_specs=(grid, rows), check_vma=False
    )
```
